256 devices in a mesh: rows: 64 (over z, x, core), samp: 4 (over y).
Axes of the slice: x: 4, y: 4, z: 8, core: 2. Of those that a mesh axis runs over, the one named last changes fastest.
Arguments:
- samples: bfloat16 [2, 32768, 2048], P(None, None, ('rows', 'samp')), may hold values from -6 to 6
- factor: bfloat16 [2, 32768, 4096], P(None, ('rows', 'samp')), as said below
- diag_inverse: bfloat16 [2, 32768, 512], P(None, 'rows'), as said below
Outputs:
- solved: float32 [2, 32768, 2048], P(None, None, ('rows', 'samp'))
The draws below stay inside these ranges and needn't reach their ends.
Inputs may be any that keep to these rules, and one draw needn't show every extreme that they name: `factor`: zero on and above the diagonal blocks: entries of rows of block b in panel k vanish unless b > k. `diag_inverse`: lower triangular within each block, diagonal between 0.5 and 1.
All inputs are finite; a program needn't handle non-finite values.
Results may differ from the reference program's by a relative error of at most 0.0065.
Values may be sent and summed in bfloat16 or wider, within the bound.
A program may use at most 128 MiB of HBM per device.

```python
import jax
import jax.numpy as jnp
from jax import lax

BLOCK = 512
BLOCKS_DEV = 2
PANELS = 8
WINDOW = 4096
SAMPLES = 2048
N_ROWS = 64


def draw_factor(key, part):
    key = jax.random.fold_in(key, 11)
    global_row = jnp.arange(BLOCKS_DEV)[:, None] * (N_ROWS * BLOCK) + jnp.arange(N_ROWS * BLOCK)[None, :]
    row_block = global_row // BLOCK
    col_block = jnp.arange(WINDOW) // BLOCK
    values_drawn = jax.random.truncated_normal(key, -4.0, 4.0, (BLOCKS_DEV, N_ROWS * BLOCK, WINDOW), jnp.float32)
    values_drawn = values_drawn * (1.5 / WINDOW ** 0.5)
    keep = row_block[:, :, None] > col_block[None, None, :]
    return jnp.where(keep, values_drawn, 0.0).astype(jnp.bfloat16)


def draw_diag_inverse(key, part):
    key = jax.random.fold_in(key, 23)
    first_key, second_key = jax.random.split(key)
    inner_row = (jnp.arange(N_ROWS * BLOCK) % BLOCK)[None, :, None]
    inner_col = jnp.arange(BLOCK)[None, None, :]
    values_drawn = jax.random.truncated_normal(first_key, -4.0, 4.0, (BLOCKS_DEV, N_ROWS * BLOCK, BLOCK), jnp.float32) * BLOCK ** (-0.5)
    diagonal = jax.random.uniform(second_key, (BLOCKS_DEV, N_ROWS * BLOCK, BLOCK), jnp.float32, 0.5, 1.0)
    result = jnp.where(inner_row > inner_col, values_drawn, 0.0)
    result = jnp.where(inner_row == inner_col, diagonal, result)
    return result.astype(jnp.bfloat16)


def steps_of(stream_key, dims, cuts, smallest, high):
    level = 1.0
    for dim, blocks in cuts:
        heights = jax.random.uniform(jax.random.fold_in(jax.random.fold_in(stream_key, 6), dim), (blocks,), jnp.float32, smallest / len(cuts), high / len(cuts))
        level = level * jnp.repeat(jnp.exp(heights), dims[dim] // blocks).reshape((-1,) + (1,) * (len(dims) - 1 - dim))
    return level


def scatter_about(rng, extent, width, limit, shards=(), kind=jnp.bfloat16):
    values = jax.random.normal(rng, extent, jnp.float32) * width
    if len(shards) > 0:
        values = steps_of(rng, extent, shards, -0.22, 0.18) * values
    return jnp.clip(values, min=-limit, max=limit).astype(kind)


def setup_inputs(seed: int = 0) -> dict:
    key_of = jax.random.split(jax.random.key(seed), 4)
    return {
        "samples": scatter_about(key_of[0], (BLOCKS_DEV, N_ROWS * BLOCK, SAMPLES), 1.0, 6.0, ((2, 256),)),
        "factor": draw_factor(jax.random.fold_in(key_of[3], 71), 0),
        "diag_inverse": draw_diag_inverse(jax.random.fold_in(key_of[3], 71), 0),
    }


def reference(samples, factor, diag_inverse):
    order_all = BLOCKS_DEV * N_ROWS * BLOCK
    working = samples.reshape(order_all, SAMPLES).astype(jnp.float32)
    lower_part = factor.reshape(order_all, WINDOW)
    inverse_rows = diag_inverse.reshape(order_all, BLOCK)
    for panel_index in range(PANELS):
        low_row = panel_index * BLOCK
        high_row = low_row + BLOCK
        solution = jnp.dot(inverse_rows[low_row:high_row].astype(jnp.float32), working[low_row:high_row], precision=lax.Precision.HIGHEST)
        working = working.at[low_row:high_row].set(solution)
        rounded = solution.astype(jnp.bfloat16).astype(jnp.float32)
        update = jnp.dot(lower_part[high_row:, low_row:high_row].astype(jnp.float32), rounded, precision=lax.Precision.HIGHEST)
        working = working.at[high_row:].add(-update)
    return working.reshape(BLOCKS_DEV, N_ROWS * BLOCK, SAMPLES)
```

```python
import functools

import jax
import jax.numpy as jnp
from jax import lax
from jax.experimental import pallas as pl
from jax.experimental.pallas import tpu as pltpu
from jax.sharding import PartitionSpec as P

MESH = pl.DeviceIdType.MESH
X_CHIPS = 4
CHUNKS = 4


def dot_nt(left, right):
    return lax.dot_general(
        left, right, (((1,), (1,)), ((), ())), preferred_element_type=jnp.float32
    )


def solve_kernel(
    n_rows, n_samp, panels, sample_ref, factor_ref, inverse_ref, out_ref,
    gathered, solved, working, inverse, factor_sem, solved_sem, send_factor, send_solved, local_sem,
):
    block = inverse.shape[0]
    columns = working.shape[1]
    chunk = columns // CHUNKS
    part = block // n_samp
    plane = 2 * X_CHIPS
    z_chips = n_rows // plane
    me, samp = lax.axis_index("rows"), lax.axis_index("samp")
    z, x, core = me // plane, (me // 2) % X_CHIPS, me % 2

    def at(z_to, x_to, core_to):
        return (z_to * X_CHIPS + x_to) * 2 + core_to

    right = at(z, (x + 1) % X_CHIPS, core)
    left = at(z, (x + X_CHIPS - 1) % X_CHIPS, core)
    above = at((z + 1) % z_chips, x, core)
    below = at((z + z_chips - 1) % z_chips, x, core)
    mate = at(z, x, 1 - core)

    barrier = pltpu.get_barrier_semaphore()
    greeted = [right, left, above, mate] + ([below] if z_chips > 2 else [])
    for other in greeted:
        pl.semaphore_signal(barrier, inc=1, device_id=(other, samp), device_id_type=MESH)
    for step in range(1, n_samp):
        pl.semaphore_signal(
            barrier, inc=1, device_id=(me, (samp + step) % n_samp), device_id_type=MESH
        )
    pl.semaphore_wait(barrier, len(greeted) + n_samp - 1)

    def gather(index, carry):
        slot, panel = index // panels, index % panels
        source = factor_ref.at[slot, :, pl.ds(pl.multiple_of(panel * block, block), block)]
        target = gathered.at[slot, panel, pl.ds(pl.multiple_of(samp * part, part), part), :]
        for step in range(1, n_samp):
            pltpu.make_async_remote_copy(
                src_ref=source, dst_ref=target, send_sem=send_factor, recv_sem=factor_sem.at[slot, panel],
                device_id=(me, (samp + step) % n_samp), device_id_type=MESH,
            ).start()
        pltpu.make_async_copy(source, target, factor_sem.at[slot, panel]).start()
        return carry

    lax.fori_loop(0, 2 * panels, gather, 0)

    in_chain = me < plane

    @pl.when(in_chain)
    def _():
        copy = pltpu.make_async_copy(inverse_ref.at[0], inverse, local_sem)
        copy.start()
        copy.wait()

    for slot in range(2):
        working[slot] = sample_ref[:, slot].astype(jnp.float32).reshape(columns, block)

    def wait_factor(slot, panel):
        whole = gathered.at[slot, panel]
        pltpu.make_async_copy(whole, whole, factor_sem.at[slot, panel]).wait()

    def item(index, carry):
        key = index // 2
        piece = key % 2 + 2 * (index % 2)
        panel = (key - piece + CHUNKS) // 2 - CHUNKS // 2
        rows = pl.ds(pl.multiple_of(piece * chunk, chunk), chunk)

        @pl.when((panel >= 0) & (panel < panels))
        def _():
            place = pl.ds(pl.multiple_of(panel * columns + piece * chunk, chunk), chunk)
            block_ref = solved.at[place]

            @pl.when(me == panel)
            def _():
                value = working[0, rows, :]
                high = value.astype(jnp.bfloat16)
                rest = value - high.astype(jnp.float32)
                middle = rest.astype(jnp.bfloat16)
                low = (rest - middle.astype(jnp.float32)).astype(jnp.bfloat16)
                product = dot_nt(jnp.concatenate([high, middle, low], axis=0), inverse[...])
                answer = product[:chunk] + (product[chunk : 2 * chunk] + product[2 * chunk :])
                working[0, rows, :] = answer
                solved[place, :] = answer.astype(jnp.bfloat16)

            @pl.when(me != panel)
            def _():
                pltpu.make_async_copy(block_ref, block_ref, solved_sem.at[panel, piece]).wait()

            def send(condition, which, other):
                @pl.when(condition)
                def _():
                    pltpu.make_async_remote_copy(
                        src_ref=block_ref, dst_ref=block_ref, send_sem=send_solved.at[which],
                        recv_sem=solved_sem.at[panel, piece], device_id=(other, samp), device_id_type=MESH,
                    ).start()

            same = core == panel % 2
            away = (x + X_CHIPS - panel // 2) % X_CHIPS
            send(same, 0, mate)
            send(same & ((away == 0) | ((away == 1) & (piece % 2 == 0))), 1, right)
            send(same & ((away == 0) | ((away == X_CHIPS - 1) & (piece % 2 == 1))), 2, left)
            send(same & (away == 0) & (z < z_chips // 2), 3, above)
            if z_chips > 2:
                send(same & (away == 0) & ((z == 0) | (z > z_chips // 2 + 1)), 4, below)

            @pl.when(in_chain & (piece == 0))
            def _():
                wait_factor(0, panel)

            @pl.when(in_chain & (me > panel))
            def _():
                working[0, rows, :] -= dot_nt(solved[place, :], gathered[0, panel])

        return carry

    lax.fori_loop(0, 2 * (2 * panels + CHUNKS - 2), item, 0)

    def update(slot):
        def body(panel, carry):
            wait_factor(slot, panel)
            whole = pl.ds(pl.multiple_of(panel * columns, columns), columns)
            working[slot] -= dot_nt(solved[whole, :], gathered[slot, panel])
            return carry

        lax.fori_loop(0, panels, body, 0)

    @pl.when(jnp.logical_not(in_chain))
    def _():
        update(0)

    update(1)
    for slot in range(2):
        out_ref[:, slot] = working[slot].reshape(n_rows, columns // n_rows, block).astype(jnp.bfloat16)

    def wait_sent(ref, sem):
        pltpu.make_async_copy(ref, ref, sem).wait()

    wait_sent(gathered.at[:, pl.ds(0, panels * (n_samp - 1) // n_samp)], send_factor)
    wait_sent(solved.at[pl.ds(0, panels // 2 * columns)], send_solved.at[0])
    for which in (1, 2):
        wait_sent(solved.at[pl.ds(0, panels // plane * 6 * chunk)], send_solved.at[which])
    column = solved.at[pl.ds(0, panels // plane * columns)]

    @pl.when(z < z_chips // 2)
    def _():
        wait_sent(column, send_solved.at[3])

    if z_chips > 2:
        @pl.when((z == 0) | (z > z_chips // 2 + 1))
        def _():
            wait_sent(column, send_solved.at[4])


def local(samples, factor, diag_inverse):
    n_rows, n_samp = lax.axis_size("rows"), lax.axis_size("samp")
    slots, order, own = samples.shape
    block = diag_inverse.shape[2]
    panels = factor.shape[2] // block
    columns = own * n_rows
    turned = samples.transpose(0, 2, 1).reshape(slots, own, n_rows, block).transpose(2, 0, 1, 3)
    regrouped = lax.all_to_all(turned, "rows", split_axis=0, concat_axis=0, tiled=True)
    result = pl.pallas_call(
        functools.partial(solve_kernel, n_rows, n_samp, panels),
        out_shape=jax.ShapeDtypeStruct((n_rows, slots, own, block), jnp.bfloat16),
        in_specs=[
            pl.BlockSpec(memory_space=pltpu.VMEM),
            pl.BlockSpec(memory_space=pl.ANY),
            pl.BlockSpec(memory_space=pl.ANY),
        ],
        out_specs=pl.BlockSpec(memory_space=pltpu.VMEM),
        scratch_shapes=[
            pltpu.VMEM((slots, panels, block, block), jnp.bfloat16),
            pltpu.VMEM((panels * columns, block), jnp.bfloat16),
            pltpu.VMEM((slots, columns, block), jnp.float32),
            pltpu.VMEM((block, block), jnp.bfloat16),
            pltpu.SemaphoreType.DMA((slots, panels)),
            pltpu.SemaphoreType.DMA((panels, CHUNKS)),
            pltpu.SemaphoreType.DMA,
            pltpu.SemaphoreType.DMA((5,)),
            pltpu.SemaphoreType.DMA,
        ],
        compiler_params=pltpu.CompilerParams(
            collective_id=0, has_side_effects=True, vmem_limit_bytes=48 * 2**20
        ),
    )(regrouped, factor, diag_inverse)
    back = lax.all_to_all(result, "rows", split_axis=0, concat_axis=0, tiled=True)
    back = back.transpose(1, 2, 0, 3).reshape(slots, own, order)
    return back.astype(jnp.float32).transpose(0, 2, 1)


def solution(mesh):
    placed = (
        P(None, None, ("rows", "samp")),
        P(None, ("rows", "samp"), None),
        P(None, "rows", None),
    )
    return jax.shard_map(
        local,
        mesh=mesh,
        in_specs=placed,
        out_specs=P(None, None, ("rows", "samp")),
        check_vma=False,
    )
```

```python
import functools

import jax
import jax.numpy as jnp
from jax import lax
from jax.experimental import pallas as pl
from jax.experimental.pallas import tpu as pltpu
from jax.sharding import PartitionSpec as P

MESH = pl.DeviceIdType.MESH
X_CHIPS = 4
CHUNKS = X_CHIPS
SLOTS = 2


def dot_nt(left, right):
    return lax.dot_general(
        left, right, (((1,), (1,)), ((), ())), preferred_element_type=jnp.float32
    )


def wait_bytes(ref, sem):
    pltpu.make_async_copy(ref, ref, sem).wait()


def solve_kernel(
    n_rows, n_samp, panels, sample_ref, factor_ref, inverse_ref, out_ref,
    gathered, solved, working, inverse, arrived, leaving, landed,
    direct_sem, near_sem, far_sem, own_sem, solved_sem, sample_sem,
    sent_direct, sent_factor, sent_mate, sent_x, sent_z, sent_sample, sent_out, out_sem, inverse_sem,
):
    block = inverse.shape[0]
    columns = working.shape[1]
    chunk = columns // CHUNKS
    part = block // n_samp
    plane = 2 * X_CHIPS
    z_chips = n_rows // plane
    me, samp = lax.axis_index("rows"), lax.axis_index("samp")
    z, x, core = me // plane, (me // 2) % X_CHIPS, me % 2
    in_chain = z == 0

    def at(z_to, x_to, core_to):
        return (z_to * X_CHIPS + x_to) * 2 + core_to

    mate = at(z, x, 1 - core)

    def remote(source, target, send_sem, recv_sem, to_rows, to_samp):
        pltpu.make_async_remote_copy(
            src_ref=source, dst_ref=target, send_sem=send_sem, recv_sem=recv_sem,
            device_id=(to_rows, to_samp), device_id_type=MESH,
        ).start()

    barrier = pltpu.get_barrier_semaphore()

    def greet(step, carry):
        pl.semaphore_signal(
            barrier, inc=1, device_id=((me + step) % n_rows, samp), device_id_type=MESH
        )
        return carry

    lax.fori_loop(1, n_rows, greet, 0)
    for step in range(1, n_samp):
        pl.semaphore_signal(
            barrier, inc=1, device_id=(me, (samp + step) % n_samp), device_id_type=MESH
        )
    pl.semaphore_wait(barrier, n_rows + n_samp - 2)

    def rows_of(index):
        return pl.ds(pl.multiple_of(index * block, block), block)

    def send_sample(slot, to):
        source, target = sample_ref.at[slot, :, rows_of(to)], arrived.at[slot, me]

        @pl.when(to != me)
        def _():
            remote(source, target, sent_sample, sample_sem.at[slot], to, samp)

        @pl.when(to == me)
        def _():
            pltpu.make_async_copy(source, target, sample_sem.at[slot]).start()

    def send_window(to, carry):
        send_sample(0, to)
        return carry

    lax.fori_loop(0, plane, send_window, 0)

    def part_of(slot, panel, owner):
        return gathered.at[slot, panel, pl.ds(pl.multiple_of(owner * part, part), part), :]

    def own_part(slot, panel):
        return factor_ref.at[slot, :, rows_of(panel)]

    def send_direct(panel, carry):
        source, target = own_part(0, panel), part_of(0, panel, samp)
        pltpu.make_async_copy(source, target, direct_sem.at[panel]).start()
        for step in range(1, n_samp):
            remote(
                source, target, sent_direct.at[panel], direct_sem.at[panel],
                me, (samp + step) % n_samp,
            )
        return carry

    def send_near(slot):
        def body(panel, carry):
            source, target = own_part(slot, panel), part_of(slot, panel, samp)
            remote(source, target, sent_factor, near_sem.at[0, slot, panel], me, (samp + 1) % n_samp)
            remote(source, target, sent_factor, near_sem.at[1, slot, panel], me, (samp + 3) % n_samp)
            pltpu.make_async_copy(source, target, own_sem.at[slot, panel]).start()
            return carry

        lax.fori_loop(0, panels, body, 0)

    def relay(slot, panel):
        before, after = (samp + 3) % n_samp, (samp + 1) % n_samp
        from_before, from_after = part_of(slot, panel, before), part_of(slot, panel, after)
        wait_bytes(from_before, near_sem.at[0, slot, panel])
        wait_bytes(from_after, near_sem.at[1, slot, panel])

        @pl.when(panel % 2 == 0)
        def _():
            remote(from_before, from_before, sent_factor, far_sem.at[slot, panel], me, after)

        @pl.when(panel % 2 == 1)
        def _():
            remote(from_after, from_after, sent_factor, far_sem.at[slot, panel], me, before)

    def relays(slot, first, count):
        def body(step, carry):
            relay(slot, first + step)
            return carry

        lax.fori_loop(0, count, body, 0)

    def panel_rows(panel):
        return pl.ds(pl.multiple_of(panel * columns, columns), columns)

    def update(slot, panel):
        wait_bytes(part_of(slot, panel, (samp + 2) % n_samp), far_sem.at[slot, panel])
        wait_bytes(part_of(slot, panel, samp), own_sem.at[slot, panel])
        working[slot] -= dot_nt(solved[panel_rows(panel), :], gathered[slot, panel])

    def take_samples(slot):
        wait_bytes(arrived.at[slot], sample_sem.at[slot])
        working[slot] = arrived[slot].astype(jnp.float32).reshape(columns, block)

    def send_rows(slot):
        leaving[slot] = working[slot].reshape(n_rows, columns // n_rows, block).astype(jnp.bfloat16)
        target = landed.at[slot, :, rows_of(me)]
        pltpu.make_async_copy(leaving.at[slot, me], target, out_sem).start()

        def body(step, carry):
            to = (me + step) % n_rows
            remote(leaving.at[slot, to], target, sent_out, out_sem, to, samp)
            return carry

        lax.fori_loop(1, n_rows, body, 0)

    @pl.when(in_chain)
    def _():
        pltpu.make_async_copy(inverse_ref.at[0], inverse, inverse_sem).start()
        lax.fori_loop(0, me, send_direct, 0)
        send_near(1)

    @pl.when(jnp.logical_not(in_chain))
    def _():
        send_near(0)

    def send_rest(step, carry):
        send_sample(0, plane + (me + step) % (n_rows - plane))
        return carry

    lax.fori_loop(0, n_rows - plane, send_rest, 0)

    def send_second(step, carry):
        send_sample(1, (me + step) % n_rows)
        return carry

    lax.fori_loop(0, n_rows, send_second, 0)

    def place_of(panel, piece):
        return pl.ds(pl.multiple_of(panel * columns + piece * chunk, chunk), chunk)

    def holds(panel, piece_x):
        return (core == panel % 2) == (piece_x == panel // 2)

    def forward(panel, piece, sem, other):
        ref = solved.at[place_of(panel, piece)]
        remote(ref, ref, sem, solved_sem.at[panel, piece], other, samp)

    def receive(panel, piece):
        wait_bytes(solved.at[place_of(panel, piece)], solved_sem.at[panel, piece])

    def chain_item(index, carry):
        key = index // 2
        piece = key % 2 + 2 * (index % 2)
        panel = (key - piece + CHUNKS) // 2 - CHUNKS // 2
        rows = pl.ds(pl.multiple_of(piece * chunk, chunk), chunk)

        @pl.when((panel >= 0) & (panel < panels))
        def _():
            place = place_of(panel, piece)

            @pl.when(me == panel)
            def _():
                value = working[0, rows, :]
                high = value.astype(jnp.bfloat16)
                rest = value - high.astype(jnp.float32)
                middle = rest.astype(jnp.bfloat16)
                low = (rest - middle.astype(jnp.float32)).astype(jnp.bfloat16)
                product = dot_nt(jnp.concatenate([high, middle, low], axis=0), inverse[...])
                answer = product[:chunk] + (product[chunk : 2 * chunk] + product[2 * chunk :])
                working[0, rows, :] = answer
                solved[place, :] = answer.astype(jnp.bfloat16)

            @pl.when(me != panel)
            def _():
                receive(panel, piece)

            holder = holds(panel, x)

            @pl.when(holder)
            def _():
                forward(panel, piece, sent_mate, mate)

            @pl.when(me == panel)
            def _():
                for step in (1, 3, 2):
                    forward(panel, piece, sent_x, at(z, (x + step) % X_CHIPS, 1 - core))

            @pl.when(holder & (piece == x))
            def _():
                for z_to in ((2, 6) if z_chips == 8 else range(1, z_chips)):
                    forward(panel, piece, sent_z, at(z_to, x, core))

            @pl.when(me > panel)
            def _():
                @pl.when(piece == 0)
                def _():
                    wait_bytes(gathered.at[0, panel], direct_sem.at[panel])

                working[0, rows, :] -= dot_nt(solved[place, :], gathered[0, panel])

        return carry

    @pl.when(in_chain)
    def _():
        wait_bytes(inverse, inverse_sem)
        take_samples(0)
        lax.fori_loop(0, 2 * (2 * panels + CHUNKS - 2), chain_item, 0)
        send_rows(0)
        relays(1, 0, panels)

    def spread_item(step, carry):
        @pl.when(step < panels)
        def _():
            panel = step

            @pl.when(holds(panel, x))
            def _():
                receive(panel, x)
                if z_chips == 8:
                    @pl.when((z == 2) | (z == 6))
                    def _():
                        forward(panel, x, sent_z, at(z - 1, x, core))
                        forward(panel, x, sent_z, at(z + 1, x, core))

                        @pl.when((panel // 2) % 2 == z // 4)
                        def _():
                            forward(panel, x, sent_z, at(4, x, core))

                for hop in (2, 1, 3):
                    forward(panel, x, sent_x, at(z, (x + hop) % X_CHIPS, core))
                forward(panel, x, sent_mate, mate)

        @pl.when(step < panels // 2)
        def _():
            relays(0, 2 * step, 2)

        @pl.when(step == panels // 2)
        def _():
            send_near(1)

        @pl.when((step >= panels - 2) & (step < panels))
        def _():
            relays(1, 2 * (step - (panels - 2)), 2)

        @pl.when(step == 1)
        def _():
            take_samples(0)

        @pl.when(step >= 1)
        def _():
            panel = step - 1
            for hop in range(1, X_CHIPS):
                piece = (x + hop) % X_CHIPS

                @pl.when(holds(panel, piece))
                def _():
                    receive(panel, piece)
                    forward(panel, piece, sent_mate, mate)

            for hop in range(X_CHIPS):
                piece = (x + hop) % X_CHIPS

                @pl.when(jnp.logical_not(holds(panel, piece)))
                def _():
                    receive(panel, piece)

            update(0, panel)

        return carry

    @pl.when(jnp.logical_not(in_chain))
    def _():
        lax.fori_loop(0, panels + 1, spread_item, 0)
        send_rows(0)
        relays(1, 4, panels - 4)

    take_samples(1)

    def update_second(panel, carry):
        update(1, panel)
        return carry

    lax.fori_loop(0, panels, update_second, 0)
    send_rows(1)

    @pl.when(in_chain)
    def _():
        def sent(panel, carry):
            wait_bytes(gathered.at[0, 0, pl.ds(0, (n_samp - 1) * part), :], sent_direct.at[panel])
            return carry

        lax.fori_loop(0, me, sent, 0)
        wait_bytes(gathered.at[1, pl.ds(0, panels * 3 // n_samp)], sent_factor)
        copies = 4 * (2 if z_chips == 8 else z_chips - 1)
        wait_bytes(solved.at[pl.ds(0, copies * chunk)], sent_z)

    @pl.when(jnp.logical_not(in_chain))
    def _():
        wait_bytes(gathered.at[:, pl.ds(0, panels * 3 // n_samp)], sent_factor)

    if z_chips == 8:
        @pl.when((z == 2) | (z == 6))
        def _():
            wait_bytes(solved.at[pl.ds(0, 10 * chunk)], sent_z)

    wait_bytes(solved.at[pl.ds(0, 16 * chunk)], sent_mate)
    wait_bytes(solved.at[pl.ds(0, 12 * chunk)], sent_x)
    wait_bytes(arrived.at[:, pl.ds(0, n_rows - 1)], sent_sample)
    wait_bytes(leaving.at[:, pl.ds(0, n_rows - 1)], sent_out)
    wait_bytes(landed, out_sem)
    out_ref[...] = landed[...]


def local(samples, factor, diag_inverse):
    n_rows, n_samp = lax.axis_size("rows"), lax.axis_size("samp")
    slots, order, own = samples.shape
    block = diag_inverse.shape[2]
    panels = factor.shape[2] // block
    columns = own * n_rows
    result = pl.pallas_call(
        functools.partial(solve_kernel, n_rows, n_samp, panels),
        out_shape=jax.ShapeDtypeStruct((slots, own, order), jnp.bfloat16),
        in_specs=[pl.BlockSpec(memory_space=pl.ANY)] * 3,
        out_specs=pl.BlockSpec(memory_space=pltpu.VMEM),
        scratch_shapes=[
            pltpu.VMEM((slots, panels, block, block), jnp.bfloat16),
            pltpu.VMEM((panels * columns, block), jnp.bfloat16),
            pltpu.VMEM((slots, columns, block), jnp.float32),
            pltpu.VMEM((block, block), jnp.bfloat16),
            pltpu.VMEM((slots, n_rows, own, block), jnp.bfloat16),
            pltpu.VMEM((slots, n_rows, own, block), jnp.bfloat16),
            pltpu.VMEM((slots, own, order), jnp.bfloat16),
            pltpu.SemaphoreType.DMA((panels,)),
            pltpu.SemaphoreType.DMA((2, slots, panels)),
            pltpu.SemaphoreType.DMA((slots, panels)),
            pltpu.SemaphoreType.DMA((slots, panels)),
            pltpu.SemaphoreType.DMA((panels, CHUNKS)),
            pltpu.SemaphoreType.DMA((slots,)),
            pltpu.SemaphoreType.DMA((panels,)),
        ]
        + [pltpu.SemaphoreType.DMA] * 8,
        compiler_params=pltpu.CompilerParams(
            collective_id=0, has_side_effects=True, vmem_limit_bytes=60 * 2**20
        ),
    )(samples.transpose(0, 2, 1), factor, diag_inverse)
    return result.astype(jnp.float32).transpose(0, 2, 1)


def solution(mesh):
    placed = (
        P(None, None, ("rows", "samp")),
        P(None, ("rows", "samp"), None),
        P(None, "rows", None),
    )
    return jax.shard_map(
        local,
        mesh=mesh,
        in_specs=placed,
        out_specs=P(None, None, ("rows", "samp")),
        check_vma=False,
    )
```

```python
import functools

import jax
import jax.numpy as jnp
from jax import lax
from jax.experimental import pallas as pl
from jax.experimental.pallas import tpu as pltpu
from jax.sharding import PartitionSpec as P

MESH = pl.DeviceIdType.MESH
X_CHIPS = 4
CHUNKS = X_CHIPS
SLOTS = 2


def dot_nt(left, right):
    return lax.dot_general(
        left, right, (((1,), (1,)), ((), ())), preferred_element_type=jnp.float32
    )


def wait_bytes(ref, sem):
    pltpu.make_async_copy(ref, ref, sem).wait()


def solve_kernel(
    n_rows, n_samp, panels, sample_ref, factor_ref, inverse_ref, out_ref,
    gathered, solved, working, inverse, arrived, leaving, landed,
    direct_sem, near_sem, far_sem, own_sem, solved_sem, share_sem, sample_sem,
    sent_direct, sent_factor, sent_mate, sent_chain, sent_share, sent_x, sent_z, sent_sample, sent_out, out_sem,
    inverse_sem,
):
    block = inverse.shape[0]
    columns = working.shape[1]
    chunk = columns // CHUNKS
    part = block // n_samp
    plane = 2 * X_CHIPS
    z_chips = n_rows // plane
    share = chunk // z_chips
    me, samp = lax.axis_index("rows"), lax.axis_index("samp")
    z, x, core = me // plane, (me // 2) % X_CHIPS, me % 2
    in_chain = z == 0

    def at(z_to, x_to, core_to):
        return (z_to * X_CHIPS + x_to) * 2 + core_to

    mate = at(z, x, 1 - core)

    def remote(source, target, send_sem, recv_sem, to_rows, to_samp):
        pltpu.make_async_remote_copy(
            src_ref=source, dst_ref=target, send_sem=send_sem, recv_sem=recv_sem,
            device_id=(to_rows, to_samp), device_id_type=MESH,
        ).start()

    barrier = pltpu.get_barrier_semaphore()

    def greet(step, carry):
        pl.semaphore_signal(
            barrier, inc=1, device_id=((me + step) % n_rows, samp), device_id_type=MESH
        )
        return carry

    lax.fori_loop(1, n_rows, greet, 0)
    for step in range(1, n_samp):
        pl.semaphore_signal(
            barrier, inc=1, device_id=(me, (samp + step) % n_samp), device_id_type=MESH
        )
    pl.semaphore_wait(barrier, n_rows + n_samp - 2)

    def rows_of(index):
        return pl.ds(pl.multiple_of(index * block, block), block)

    def send_sample(slot, to):
        source, target = sample_ref.at[slot, :, rows_of(to)], arrived.at[slot, me]

        @pl.when(to != me)
        def _():
            remote(source, target, sent_sample, sample_sem.at[slot], to, samp)

        @pl.when(to == me)
        def _():
            pltpu.make_async_copy(source, target, sample_sem.at[slot]).start()

    def send_window(to, carry):
        send_sample(0, to)
        return carry

    lax.fori_loop(0, plane, send_window, 0)

    def part_of(slot, panel, owner):
        return gathered.at[slot, panel, pl.ds(pl.multiple_of(owner * part, part), part), :]

    def own_part(slot, panel):
        return factor_ref.at[slot, :, rows_of(panel)]

    def send_direct(panel, carry):
        source, target = own_part(0, panel), part_of(0, panel, samp)
        pltpu.make_async_copy(source, target, direct_sem.at[panel]).start()
        for step in range(1, n_samp):
            remote(
                source, target, sent_direct.at[panel], direct_sem.at[panel],
                me, (samp + step) % n_samp,
            )
        return carry

    def send_near(slot):
        def body(panel, carry):
            source, target = own_part(slot, panel), part_of(slot, panel, samp)
            remote(source, target, sent_factor, near_sem.at[0, slot, panel], me, (samp + 1) % n_samp)
            remote(source, target, sent_factor, near_sem.at[1, slot, panel], me, (samp + 3) % n_samp)
            pltpu.make_async_copy(source, target, own_sem.at[slot, panel]).start()
            return carry

        lax.fori_loop(0, panels, body, 0)

    def relay(slot, panel):
        before, after = (samp + 3) % n_samp, (samp + 1) % n_samp
        from_before, from_after = part_of(slot, panel, before), part_of(slot, panel, after)
        wait_bytes(from_before, near_sem.at[0, slot, panel])
        wait_bytes(from_after, near_sem.at[1, slot, panel])

        @pl.when(panel % 2 == 0)
        def _():
            remote(from_before, from_before, sent_factor, far_sem.at[slot, panel], me, after)

        @pl.when(panel % 2 == 1)
        def _():
            remote(from_after, from_after, sent_factor, far_sem.at[slot, panel], me, before)

    def relays(slot, first, count):
        def body(step, carry):
            relay(slot, first + step)
            return carry

        lax.fori_loop(0, count, body, 0)

    def panel_rows(panel):
        return pl.ds(pl.multiple_of(panel * columns, columns), columns)

    def update(slot, panel):
        wait_bytes(part_of(slot, panel, (samp + 2) % n_samp), far_sem.at[slot, panel])
        wait_bytes(part_of(slot, panel, samp), own_sem.at[slot, panel])
        working[slot] -= dot_nt(solved[panel_rows(panel), :], gathered[slot, panel])

    def take_samples(slot):
        wait_bytes(arrived.at[slot], sample_sem.at[slot])
        working[slot] = arrived[slot].astype(jnp.float32).reshape(columns, block)

    def send_rows(slot):
        leaving[slot] = working[slot].reshape(n_rows, columns // n_rows, block).astype(jnp.bfloat16)
        target = landed.at[slot, :, rows_of(me)]
        pltpu.make_async_copy(leaving.at[slot, me], target, out_sem).start()

        def body(step, carry):
            to = (me + step) % n_rows
            remote(leaving.at[slot, to], target, sent_out, out_sem, to, samp)
            return carry

        lax.fori_loop(1, n_rows, body, 0)

    @pl.when(in_chain)
    def _():
        pltpu.make_async_copy(inverse_ref.at[0], inverse, inverse_sem).start()
        lax.fori_loop(0, me, send_direct, 0)
        send_near(1)

    @pl.when(jnp.logical_not(in_chain))
    def _():
        send_near(0)

    def send_rest(step, carry):
        send_sample(0, plane + (me + step) % (n_rows - plane))
        return carry

    lax.fori_loop(0, n_rows - plane, send_rest, 0)

    def send_second(step, carry):
        send_sample(1, (me + step) % n_rows)
        return carry

    lax.fori_loop(0, n_rows, send_second, 0)

    def place_of(panel, piece):
        return pl.ds(pl.multiple_of(panel * columns + piece * chunk, chunk), chunk)

    def forward(panel, piece, sem, other):
        ref = solved.at[place_of(panel, piece)]
        remote(ref, ref, sem, solved_sem.at[panel, piece], other, samp)

    def forward_share(panel, piece, index, send_sem, recv_sem, other):
        start = panel * columns + piece * chunk + index * share
        ref = solved.at[pl.ds(pl.multiple_of(start, share), share)]
        remote(ref, ref, send_sem, recv_sem, other, samp)

    def receive(panel, piece):
        wait_bytes(solved.at[place_of(panel, piece)], solved_sem.at[panel, piece])

    def chain_item(index, carry):
        key = index // 2
        piece = key % 2 + 2 * (index % 2)
        panel = (key - piece + CHUNKS) // 2 - CHUNKS // 2
        rows = pl.ds(pl.multiple_of(piece * chunk, chunk), chunk)

        @pl.when((panel >= 0) & (panel < 2 * x + 2))
        def _():
            place = place_of(panel, piece)
            owner_x, owner_core = panel // 2, panel % 2

            @pl.when(me == panel)
            def _():
                value = working[0, rows, :]
                high = value.astype(jnp.bfloat16)
                rest = value - high.astype(jnp.float32)
                middle = rest.astype(jnp.bfloat16)
                low = (rest - middle.astype(jnp.float32)).astype(jnp.bfloat16)
                product = dot_nt(jnp.concatenate([high, middle, low], axis=0), inverse[...])
                answer = product[:chunk] + (product[chunk : 2 * chunk] + product[2 * chunk :])
                working[0, rows, :] = answer
                solved[place, :] = answer.astype(jnp.bfloat16)

            @pl.when(me != panel)
            def _():
                receive(panel, piece)

            @pl.when((me == panel) | ((core == 0) & (owner_x < x)))
            def _():
                forward(panel, piece, sent_mate, mate)

            @pl.when((me == panel) & (core == 1))
            def _():
                for ahead in (1, 3, 2):
                    @pl.when(x + ahead < X_CHIPS)
                    def _():
                        forward(panel - 1, piece, sent_chain, at(z, x + ahead, 0))
                        forward(panel, piece, sent_chain, at(z, x + ahead, 0))

            @pl.when(me == panel)
            def _():
                for z_to in range(1, z_chips):
                    forward_share(
                        panel, piece, z_to, sent_share, share_sem.at[panel], at(z_to, piece, core)
                    )

                @pl.when(piece < x)
                def _():
                    forward_share(panel, piece, 0, sent_share, share_sem.at[panel], at(0, piece, core))

            @pl.when((piece == x) & (core == owner_core))
            def _():
                for z_to in range(1, z_chips):
                    forward_share(
                        panel, piece, 0, sent_z, solved_sem.at[panel, piece], at(z_to, x, core)
                    )
                for x_to in range(X_CHIPS - 1):
                    @pl.when(x_to < owner_x)
                    def _():
                        forward(panel, piece, sent_x, at(z, x_to, core))

            @pl.when(me > panel)
            def _():
                @pl.when(piece == 0)
                def _():
                    wait_bytes(gathered.at[0, panel], direct_sem.at[panel])

                working[0, rows, :] -= dot_nt(solved[place, :], gathered[0, panel])

        return carry

    def spread_item(step, carry):
        first = jnp.where(in_chain, 2 * x + 2, 0)

        def with_panel(lag, body):
            panel = step - lag

            @pl.when((panel >= first) & (panel < panels))
            def _():
                body(panel, core == panel % 2, panel // 2)

        def give_share(panel, mine, owner_x):
            @pl.when(mine)
            def _():
                wait_bytes(solved.at[pl.ds(0, share)], share_sem.at[panel])
                for hop in range(1, z_chips):
                    z_to = (z + hop) % z_chips

                    @pl.when((z_to > 0) | (x < owner_x))
                    def _():
                        forward_share(
                            panel, x, z, sent_z, solved_sem.at[panel, x], at(z_to, x, core)
                        )

        def give_chunk(panel, mine, owner_x):
            @pl.when(mine)
            def _():
                wait_bytes(solved.at[pl.ds(0, chunk - share)], solved_sem.at[panel, x])
                for hop in (2, 1, 3):
                    x_to = (x + hop) % X_CHIPS

                    @pl.when((z > 0) | (x_to < owner_x))
                    def _():
                        forward(panel, x, sent_x, at(z, x_to, core))

                forward(panel, x, sent_mate, mate)

        def take_rest(panel, mine, owner_x):
            for hop in range(1, X_CHIPS):
                piece = (x + hop) % X_CHIPS
                receive(panel, piece)

                @pl.when(mine)
                def _():
                    forward(panel, piece, sent_mate, mate)

            @pl.when(jnp.logical_not(mine))
            def _():
                receive(panel, x)

            @pl.when(z > 0)
            def _():
                update(0, panel)

        with_panel(0, give_share)
        with_panel(1, give_chunk)

        @pl.when(z > 0)
        def _():
            @pl.when(step < panels // 2)
            def _():
                relays(0, 2 * step, 2)

            @pl.when(step == panels // 2)
            def _():
                send_near(1)

            @pl.when((step >= panels - 2) & (step < panels))
            def _():
                relays(1, 2 * (step - (panels - 2)), 2)

            @pl.when(step == 2)
            def _():
                take_samples(0)

        with_panel(2, take_rest)
        return carry

    @pl.when(in_chain)
    def _():
        wait_bytes(inverse, inverse_sem)
        take_samples(0)
        lax.fori_loop(0, 2 * (4 * x + CHUNKS + 2), chain_item, 0)

    lax.fori_loop(0, panels + 2, spread_item, 0)
    send_rows(0)

    @pl.when(in_chain)
    def _():
        relays(1, 0, panels)

    @pl.when(jnp.logical_not(in_chain))
    def _():
        relays(1, 4, panels - 4)

    take_samples(1)

    def update_second(panel, carry):
        update(1, panel)
        return carry

    lax.fori_loop(0, panels, update_second, 0)
    send_rows(1)

    @pl.when(in_chain)
    def _():
        def sent(panel, carry):
            wait_bytes(gathered.at[0, 0, pl.ds(0, (n_samp - 1) * part), :], sent_direct.at[panel])
            return carry

        lax.fori_loop(0, me, sent, 0)
        wait_bytes(gathered.at[1, pl.ds(0, panels * 3 // n_samp)], sent_factor)

    def wait_rows(condition, rows, sem):
        if rows > 0:
            @pl.when(condition)
            def _():
                wait_bytes(solved.at[pl.ds(0, rows)], sem)

    wait_rows(z > 0, 16 * chunk, sent_mate)
    wait_rows(z > 0, 12 * chunk, sent_x)
    wait_rows(z == 0, 4 * (z_chips - 1) * share, sent_z)
    for place in range(X_CHIPS):
        here = in_chain & (x == place)
        wait_rows(here & (core == 0), 4 * (4 + place) * chunk, sent_mate)
        wait_rows(here & (core == 1), 4 * (4 - place) * chunk, sent_mate)
        wait_rows(here & (core == 1), 8 * (3 - place) * chunk, sent_chain)
        wait_rows(here, (3 + place) * chunk, sent_x)
        wait_rows(here, (4 * (z_chips - 1) + place) * share, sent_share)
        others = (z_chips - 1) * (3 - place) + (z_chips - 2) * (place + 1)
        wait_rows((z > 0) & (x == place), others * share, sent_z)

    @pl.when(jnp.logical_not(in_chain))
    def _():
        wait_bytes(gathered.at[:, pl.ds(0, panels * 3 // n_samp)], sent_factor)

    wait_bytes(arrived.at[:, pl.ds(0, n_rows - 1)], sent_sample)
    wait_bytes(leaving.at[:, pl.ds(0, n_rows - 1)], sent_out)
    wait_bytes(landed, out_sem)
    out_ref[...] = landed[...]


def local(samples, factor, diag_inverse):
    n_rows, n_samp = lax.axis_size("rows"), lax.axis_size("samp")
    slots, order, own = samples.shape
    block = diag_inverse.shape[2]
    panels = factor.shape[2] // block
    columns = own * n_rows
    result = pl.pallas_call(
        functools.partial(solve_kernel, n_rows, n_samp, panels),
        out_shape=jax.ShapeDtypeStruct((slots, own, order), jnp.bfloat16),
        in_specs=[pl.BlockSpec(memory_space=pl.ANY)] * 3,
        out_specs=pl.BlockSpec(memory_space=pltpu.VMEM),
        scratch_shapes=[
            pltpu.VMEM((slots, panels, block, block), jnp.bfloat16),
            pltpu.VMEM((panels * columns, block), jnp.bfloat16),
            pltpu.VMEM((slots, columns, block), jnp.float32),
            pltpu.VMEM((block, block), jnp.bfloat16),
            pltpu.VMEM((slots, n_rows, own, block), jnp.bfloat16),
            pltpu.VMEM((slots, n_rows, own, block), jnp.bfloat16),
            pltpu.VMEM((slots, own, order), jnp.bfloat16),
            pltpu.SemaphoreType.DMA((panels,)),
            pltpu.SemaphoreType.DMA((2, slots, panels)),
            pltpu.SemaphoreType.DMA((slots, panels)),
            pltpu.SemaphoreType.DMA((slots, panels)),
            pltpu.SemaphoreType.DMA((panels, CHUNKS)),
            pltpu.SemaphoreType.DMA((panels,)),
            pltpu.SemaphoreType.DMA((slots,)),
            pltpu.SemaphoreType.DMA((panels,)),
        ]
        + [pltpu.SemaphoreType.DMA] * 10,
        compiler_params=pltpu.CompilerParams(
            collective_id=0, has_side_effects=True, vmem_limit_bytes=60 * 2**20
        ),
    )(samples.transpose(0, 2, 1), factor, diag_inverse)
    return result.astype(jnp.float32).transpose(0, 2, 1)


def solution(mesh):
    placed = (
        P(None, None, ("rows", "samp")),
        P(None, ("rows", "samp"), None),
        P(None, "rows", None),
    )
    return jax.shard_map(
        local,
        mesh=mesh,
        in_specs=placed,
        out_specs=P(None, None, ("rows", "samp")),
        check_vma=False,
    )
```

```python
import functools

import jax
import jax.numpy as jnp
from jax import lax
from jax.experimental import pallas as pl
from jax.experimental.pallas import tpu as pltpu
from jax.sharding import PartitionSpec as P

MESH = pl.DeviceIdType.MESH
X_CHIPS = 4
CHUNKS = X_CHIPS
SLOTS = 2


def dot_nt(left, right):
    return lax.dot_general(
        left, right, (((1,), (1,)), ((), ())), preferred_element_type=jnp.float32
    )


def wait_bytes(ref, sem):
    pltpu.make_async_copy(ref, ref, sem).wait()


def solve_kernel(
    n_rows, n_samp, panels, sample_ref, factor_ref, inverse_ref, out_ref,
    gathered, solved, working, inverse, arrived, leaving, landed,
    direct_sem, near_sem, far_sem, own_sem, solved_sem, share_sem, sample_sem,
    sent_direct, sent_factor, sent_mate, sent_chain, sent_share, sent_x, sent_z, sent_sample, sent_out, out_sem,
    inverse_sem,
):
    block = inverse.shape[0]
    columns = working.shape[1]
    chunk = columns // CHUNKS
    part = block // n_samp
    plane = 2 * X_CHIPS
    z_chips = n_rows // plane
    share = chunk // z_chips
    me, samp = lax.axis_index("rows"), lax.axis_index("samp")
    z, x, core = me // plane, (me // 2) % X_CHIPS, me % 2
    in_chain = z == 0

    def at(z_to, x_to, core_to):
        return (z_to * X_CHIPS + x_to) * 2 + core_to

    mate = at(z, x, 1 - core)

    def remote(source, target, send_sem, recv_sem, to_rows, to_samp):
        pltpu.make_async_remote_copy(
            src_ref=source, dst_ref=target, send_sem=send_sem, recv_sem=recv_sem,
            device_id=(to_rows, to_samp), device_id_type=MESH,
        ).start()

    barrier = pltpu.get_barrier_semaphore()

    def greet(step, carry):
        pl.semaphore_signal(
            barrier, inc=1, device_id=((me + step) % n_rows, samp), device_id_type=MESH
        )
        return carry

    lax.fori_loop(1, n_rows, greet, 0)
    for step in range(1, n_samp):
        pl.semaphore_signal(
            barrier, inc=1, device_id=(me, (samp + step) % n_samp), device_id_type=MESH
        )
    pl.semaphore_wait(barrier, n_rows + n_samp - 2)

    def rows_of(index):
        return pl.ds(pl.multiple_of(index * block, block), block)

    def send_sample(slot, to):
        source, target = sample_ref.at[slot, :, rows_of(to)], arrived.at[slot, me]

        @pl.when(to != me)
        def _():
            remote(source, target, sent_sample, sample_sem.at[slot], to, samp)

        @pl.when(to == me)
        def _():
            pltpu.make_async_copy(source, target, sample_sem.at[slot]).start()

    def send_window(to, carry):
        send_sample(0, to)
        return carry

    lax.fori_loop(0, plane, send_window, 0)

    def part_of(slot, panel, owner):
        return gathered.at[slot, panel, pl.ds(pl.multiple_of(owner * part, part), part), :]

    def own_part(slot, panel):
        return factor_ref.at[slot, :, rows_of(panel)]

    def send_direct(panel, carry):
        source, target = own_part(0, panel), part_of(0, panel, samp)
        pltpu.make_async_copy(source, target, direct_sem.at[panel]).start()
        for step in range(1, n_samp):
            remote(
                source, target, sent_direct.at[panel], direct_sem.at[panel],
                me, (samp + step) % n_samp,
            )
        return carry

    def send_near(slot):
        def body(panel, carry):
            source, target = own_part(slot, panel), part_of(slot, panel, samp)
            remote(source, target, sent_factor, near_sem.at[0, slot, panel], me, (samp + 1) % n_samp)
            remote(source, target, sent_factor, near_sem.at[1, slot, panel], me, (samp + 3) % n_samp)
            pltpu.make_async_copy(source, target, own_sem.at[slot, panel]).start()
            return carry

        lax.fori_loop(0, panels, body, 0)

    def relay(slot, panel):
        before, after = (samp + 3) % n_samp, (samp + 1) % n_samp
        from_before, from_after = part_of(slot, panel, before), part_of(slot, panel, after)
        wait_bytes(from_before, near_sem.at[0, slot, panel])
        wait_bytes(from_after, near_sem.at[1, slot, panel])

        @pl.when(panel % 2 == 0)
        def _():
            remote(from_before, from_before, sent_factor, far_sem.at[slot, panel], me, after)

        @pl.when(panel % 2 == 1)
        def _():
            remote(from_after, from_after, sent_factor, far_sem.at[slot, panel], me, before)

    def relays(slot, first, count):
        def body(step, carry):
            relay(slot, first + step)
            return carry

        lax.fori_loop(0, count, body, 0)

    def panel_rows(panel):
        return pl.ds(pl.multiple_of(panel * columns, columns), columns)

    def update(slot, panel):
        wait_bytes(part_of(slot, panel, (samp + 2) % n_samp), far_sem.at[slot, panel])
        wait_bytes(part_of(slot, panel, samp), own_sem.at[slot, panel])
        working[slot] -= dot_nt(solved[panel_rows(panel), :], gathered[slot, panel])

    def take_samples(slot):
        wait_bytes(arrived.at[slot], sample_sem.at[slot])
        working[slot] = arrived[slot].astype(jnp.float32).reshape(columns, block)

    def send_rows(slot):
        leaving[slot] = working[slot].reshape(n_rows, columns // n_rows, block).astype(jnp.bfloat16)
        target = landed.at[slot, :, rows_of(me)]
        pltpu.make_async_copy(leaving.at[slot, me], target, out_sem).start()

        def body(step, carry):
            to = (me + step) % n_rows
            remote(leaving.at[slot, to], target, sent_out, out_sem, to, samp)
            return carry

        lax.fori_loop(1, n_rows, body, 0)

    @pl.when(in_chain)
    def _():
        pltpu.make_async_copy(inverse_ref.at[0], inverse, inverse_sem).start()
        lax.fori_loop(0, me, send_direct, 0)
        send_near(1)

    @pl.when(jnp.logical_not(in_chain))
    def _():
        send_near(0)

    def send_rest(step, carry):
        send_sample(0, plane + (me + step) % (n_rows - plane))
        return carry

    lax.fori_loop(0, n_rows - plane, send_rest, 0)

    def send_second(step, carry):
        send_sample(1, (me + step) % n_rows)
        return carry

    lax.fori_loop(0, n_rows, send_second, 0)

    def place_of(panel, piece):
        return pl.ds(pl.multiple_of(panel * columns + piece * chunk, chunk), chunk)

    def forward(panel, piece, sem, other):
        ref = solved.at[place_of(panel, piece)]
        remote(ref, ref, sem, solved_sem.at[panel, piece], other, samp)

    def forward_share(panel, piece, index, send_sem, recv_sem, other):
        start = panel * columns + piece * chunk + index * share
        ref = solved.at[pl.ds(pl.multiple_of(start, share), share)]
        remote(ref, ref, send_sem, recv_sem, other, samp)

    def receive(panel, piece):
        wait_bytes(solved.at[place_of(panel, piece)], solved_sem.at[panel, piece])

    def chain_item(index, carry):
        owner_x = x - (index // 2) % (x + 1)
        piece = (index // 2) // (x + 1) - owner_x
        panel = 2 * owner_x + index % 2
        rows = pl.ds(pl.multiple_of(piece * chunk, chunk), chunk)

        @pl.when((piece >= 0) & (piece < CHUNKS) & (panel <= me))
        def _():
            place = place_of(panel, piece)
            owner_core = panel % 2

            @pl.when(me == panel)
            def _():
                value = working[0, rows, :]
                high = value.astype(jnp.bfloat16)
                rest = value - high.astype(jnp.float32)
                middle = rest.astype(jnp.bfloat16)
                low = (rest - middle.astype(jnp.float32)).astype(jnp.bfloat16)
                product = dot_nt(jnp.concatenate([high, middle, low], axis=0), inverse[...])
                answer = product[:chunk] + (product[chunk : 2 * chunk] + product[2 * chunk :])
                working[0, rows, :] = answer
                solved[place, :] = answer.astype(jnp.bfloat16)

            @pl.when(me != panel)
            def _():
                receive(panel, piece)

            @pl.when((me == panel) | ((core == 0) & (owner_x < x)))
            def _():
                forward(panel, piece, sent_mate, mate)

            @pl.when((me == panel) & (core == 1))
            def _():
                for ahead in (1, 3, 2):
                    @pl.when(x + ahead < X_CHIPS)
                    def _():
                        forward(panel - 1, piece, sent_chain, at(z, x + ahead, 0))
                        forward(panel, piece, sent_chain, at(z, x + ahead, 0))

            @pl.when(me == panel)
            def _():
                for z_to in range(1, z_chips):
                    forward_share(
                        panel, piece, z_to, sent_share, share_sem.at[panel], at(z_to, piece, core)
                    )

                @pl.when(piece < x)
                def _():
                    forward_share(panel, piece, 0, sent_share, share_sem.at[panel], at(0, piece, core))

            @pl.when((piece == x) & (core == owner_core))
            def _():
                for z_to in range(1, z_chips):
                    forward_share(
                        panel, piece, 0, sent_z, solved_sem.at[panel, piece], at(z_to, x, core)
                    )
                for x_to in range(X_CHIPS - 1):
                    @pl.when(x_to < owner_x)
                    def _():
                        forward(panel, piece, sent_x, at(z, x_to, core))

            @pl.when(me > panel)
            def _():
                @pl.when(piece == 0)
                def _():
                    wait_bytes(gathered.at[0, panel], direct_sem.at[panel])

                working[0, rows, :] -= dot_nt(solved[place, :], gathered[0, panel])

        return carry

    def spread_item(step, carry):
        first = jnp.where(in_chain, 2 * x + 2, 0)

        def with_panel(lag, body):
            panel = step - lag

            @pl.when((panel >= first) & (panel < panels))
            def _():
                body(panel, core == panel % 2, panel // 2)

        def give_share(panel, mine, owner_x):
            @pl.when(mine)
            def _():
                wait_bytes(solved.at[pl.ds(0, share)], share_sem.at[panel])
                for hop in range(1, z_chips):
                    z_to = (z + hop) % z_chips

                    @pl.when((z_to > 0) | (x < owner_x))
                    def _():
                        forward_share(
                            panel, x, z, sent_z, solved_sem.at[panel, x], at(z_to, x, core)
                        )

        def give_chunk(panel, mine, owner_x):
            @pl.when(mine)
            def _():
                wait_bytes(solved.at[pl.ds(0, chunk - share)], solved_sem.at[panel, x])
                for hop in (2, 1, 3):
                    x_to = (x + hop) % X_CHIPS

                    @pl.when((z > 0) | (x_to < owner_x))
                    def _():
                        forward(panel, x, sent_x, at(z, x_to, core))

                forward(panel, x, sent_mate, mate)

        def take_rest(panel, mine, owner_x):
            for hop in range(1, X_CHIPS):
                piece = (x + hop) % X_CHIPS
                receive(panel, piece)

                @pl.when(mine)
                def _():
                    forward(panel, piece, sent_mate, mate)

            @pl.when(jnp.logical_not(mine))
            def _():
                receive(panel, x)

            @pl.when(z > 0)
            def _():
                update(0, panel)

        with_panel(0, give_share)
        with_panel(1, give_chunk)

        @pl.when(z > 0)
        def _():
            @pl.when(step < panels // 2)
            def _():
                relays(0, 2 * step, 2)

            @pl.when(step == panels // 2)
            def _():
                send_near(1)

            @pl.when((step >= panels - 2) & (step < panels))
            def _():
                relays(1, 2 * (step - (panels - 2)), 2)

            @pl.when(step == 2)
            def _():
                take_samples(0)

        with_panel(2, take_rest)
        return carry

    @pl.when(in_chain)
    def _():
        wait_bytes(inverse, inverse_sem)
        take_samples(0)
        lax.fori_loop(0, 2 * (x + CHUNKS) * (x + 1), chain_item, 0)

        @pl.when(core == 0)
        def _():
            for piece in range(CHUNKS):
                receive(me + 1, piece)

    lax.fori_loop(0, panels + 2, spread_item, 0)
    send_rows(0)

    @pl.when(in_chain)
    def _():
        relays(1, 0, panels)

    @pl.when(jnp.logical_not(in_chain))
    def _():
        relays(1, 4, panels - 4)

    take_samples(1)

    def update_second(panel, carry):
        update(1, panel)
        return carry

    lax.fori_loop(0, panels, update_second, 0)
    send_rows(1)

    @pl.when(in_chain)
    def _():
        def sent(panel, carry):
            wait_bytes(gathered.at[0, 0, pl.ds(0, (n_samp - 1) * part), :], sent_direct.at[panel])
            return carry

        lax.fori_loop(0, me, sent, 0)
        wait_bytes(gathered.at[1, pl.ds(0, panels * 3 // n_samp)], sent_factor)

    def wait_rows(condition, rows, sem):
        if rows > 0:
            @pl.when(condition)
            def _():
                wait_bytes(solved.at[pl.ds(0, rows)], sem)

    wait_rows(z > 0, 16 * chunk, sent_mate)
    wait_rows(z > 0, 12 * chunk, sent_x)
    wait_rows(z == 0, 4 * (z_chips - 1) * share, sent_z)
    for place in range(X_CHIPS):
        here = in_chain & (x == place)
        wait_rows(here & (core == 0), 4 * (4 + place) * chunk, sent_mate)
        wait_rows(here & (core == 1), 4 * (4 - place) * chunk, sent_mate)
        wait_rows(here & (core == 1), 8 * (3 - place) * chunk, sent_chain)
        wait_rows(here, (3 + place) * chunk, sent_x)
        wait_rows(here, (4 * (z_chips - 1) + place) * share, sent_share)
        others = (z_chips - 1) * (3 - place) + (z_chips - 2) * (place + 1)
        wait_rows((z > 0) & (x == place), others * share, sent_z)

    @pl.when(jnp.logical_not(in_chain))
    def _():
        wait_bytes(gathered.at[:, pl.ds(0, panels * 3 // n_samp)], sent_factor)

    wait_bytes(arrived.at[:, pl.ds(0, n_rows - 1)], sent_sample)
    wait_bytes(leaving.at[:, pl.ds(0, n_rows - 1)], sent_out)
    wait_bytes(landed, out_sem)
    out_ref[...] = landed[...]


def local(samples, factor, diag_inverse):
    n_rows, n_samp = lax.axis_size("rows"), lax.axis_size("samp")
    slots, order, own = samples.shape
    block = diag_inverse.shape[2]
    panels = factor.shape[2] // block
    columns = own * n_rows
    result = pl.pallas_call(
        functools.partial(solve_kernel, n_rows, n_samp, panels),
        out_shape=jax.ShapeDtypeStruct((slots, own, order), jnp.bfloat16),
        in_specs=[pl.BlockSpec(memory_space=pl.ANY)] * 3,
        out_specs=pl.BlockSpec(memory_space=pltpu.VMEM),
        scratch_shapes=[
            pltpu.VMEM((slots, panels, block, block), jnp.bfloat16),
            pltpu.VMEM((panels * columns, block), jnp.bfloat16),
            pltpu.VMEM((slots, columns, block), jnp.float32),
            pltpu.VMEM((block, block), jnp.bfloat16),
            pltpu.VMEM((slots, n_rows, own, block), jnp.bfloat16),
            pltpu.VMEM((slots, n_rows, own, block), jnp.bfloat16),
            pltpu.VMEM((slots, own, order), jnp.bfloat16),
            pltpu.SemaphoreType.DMA((panels,)),
            pltpu.SemaphoreType.DMA((2, slots, panels)),
            pltpu.SemaphoreType.DMA((slots, panels)),
            pltpu.SemaphoreType.DMA((slots, panels)),
            pltpu.SemaphoreType.DMA((panels, CHUNKS)),
            pltpu.SemaphoreType.DMA((panels,)),
            pltpu.SemaphoreType.DMA((slots,)),
            pltpu.SemaphoreType.DMA((panels,)),
        ]
        + [pltpu.SemaphoreType.DMA] * 10,
        compiler_params=pltpu.CompilerParams(
            collective_id=0, has_side_effects=True, vmem_limit_bytes=60 * 2**20
        ),
    )(samples.transpose(0, 2, 1), factor, diag_inverse)
    return result.astype(jnp.float32).transpose(0, 2, 1)


def solution(mesh):
    placed = (
        P(None, None, ("rows", "samp")),
        P(None, ("rows", "samp"), None),
        P(None, "rows", None),
    )
    return jax.shard_map(
        local,
        mesh=mesh,
        in_specs=placed,
        out_specs=P(None, None, ("rows", "samp")),
        check_vma=False,
    )
```

```python
import functools

import jax
import jax.numpy as jnp
from jax import lax
from jax.experimental import pallas as pl
from jax.experimental.pallas import tpu as pltpu
from jax.sharding import PartitionSpec as P

MESH = pl.DeviceIdType.MESH
X_CHIPS = 4
CHUNKS = X_CHIPS
SLOTS = 2


def dot_nt(left, right):
    return lax.dot_general(
        left, right, (((1,), (1,)), ((), ())), preferred_element_type=jnp.float32
    )


def wait_bytes(ref, sem):
    pltpu.make_async_copy(ref, ref, sem).wait()


def solve_kernel(
    n_rows, n_samp, panels, sample_ref, factor_ref, inverse_ref, out_ref,
    gathered, solved, working, inverse, arrived, leaving, landed,
    direct_sem, near_sem, far_sem, own_sem, solved_sem, share_sem, sample_sem,
    sent_direct, sent_factor, sent_mate, sent_chain, sent_share, sent_x, sent_z, sent_sample, sent_out, out_sem,
    inverse_sem,
):
    block = inverse.shape[0]
    columns = working.shape[1]
    chunk = columns // CHUNKS
    part = block // n_samp
    plane = 2 * X_CHIPS
    z_chips = n_rows // plane
    share = chunk // z_chips
    me, samp = lax.axis_index("rows"), lax.axis_index("samp")
    z, x, core = me // plane, (me // 2) % X_CHIPS, me % 2
    in_chain = z == 0

    def at(z_to, x_to, core_to):
        return (z_to * X_CHIPS + x_to) * 2 + core_to

    mate = at(z, x, 1 - core)
    ring = 2 * z_chips
    group = x * ring + z * 2 + core

    def remote(source, target, send_sem, recv_sem, to_rows, to_samp):
        pltpu.make_async_remote_copy(
            src_ref=source, dst_ref=target, send_sem=send_sem, recv_sem=recv_sem,
            device_id=(to_rows, to_samp), device_id_type=MESH,
        ).start()

    barrier = pltpu.get_barrier_semaphore()

    def greet(step, carry):
        pl.semaphore_signal(
            barrier, inc=1, device_id=((me + step) % n_rows, samp), device_id_type=MESH
        )
        return carry

    lax.fori_loop(1, n_rows, greet, 0)
    for step in range(1, n_samp):
        pl.semaphore_signal(
            barrier, inc=1, device_id=(me, (samp + step) % n_samp), device_id_type=MESH
        )
    pl.semaphore_wait(barrier, n_rows + n_samp - 2)

    def rows_of(index):
        return pl.ds(pl.multiple_of(index * block, block), block)

    def send_sample(slot, to):
        source, target = sample_ref.at[slot, :, rows_of(to)], arrived.at[slot, group]

        @pl.when(to != me)
        def _():
            remote(source, target, sent_sample, sample_sem.at[slot], to, samp)

        @pl.when(to == me)
        def _():
            pltpu.make_async_copy(source, target, sample_sem.at[slot]).start()

    def send_window(to, carry):
        send_sample(0, to)
        return carry

    lax.fori_loop(0, plane, send_window, 0)

    def part_of(slot, panel, owner):
        return gathered.at[slot, panel, pl.ds(pl.multiple_of(owner * part, part), part), :]

    def own_part(slot, panel):
        return factor_ref.at[slot, :, rows_of(panel)]

    def send_direct(panel, carry):
        source, target = own_part(0, panel), part_of(0, panel, samp)
        pltpu.make_async_copy(source, target, direct_sem.at[panel]).start()
        for step in range(1, n_samp):
            remote(
                source, target, sent_direct.at[panel], direct_sem.at[panel],
                me, (samp + step) % n_samp,
            )
        return carry

    def send_near(slot):
        def body(panel, carry):
            source, target = own_part(slot, panel), part_of(slot, panel, samp)
            remote(source, target, sent_factor, near_sem.at[0, slot, panel], me, (samp + 1) % n_samp)
            remote(source, target, sent_factor, near_sem.at[1, slot, panel], me, (samp + 3) % n_samp)
            pltpu.make_async_copy(source, target, own_sem.at[slot, panel]).start()
            return carry

        lax.fori_loop(0, panels, body, 0)

    def relay(slot, panel):
        before, after = (samp + 3) % n_samp, (samp + 1) % n_samp
        from_before, from_after = part_of(slot, panel, before), part_of(slot, panel, after)
        wait_bytes(from_before, near_sem.at[0, slot, panel])
        wait_bytes(from_after, near_sem.at[1, slot, panel])

        @pl.when(panel % 2 == 0)
        def _():
            remote(from_before, from_before, sent_factor, far_sem.at[slot, panel], me, after)

        @pl.when(panel % 2 == 1)
        def _():
            remote(from_after, from_after, sent_factor, far_sem.at[slot, panel], me, before)

    def relays(slot, first, count):
        def body(step, carry):
            relay(slot, first + step)
            return carry

        lax.fori_loop(0, count, body, 0)

    def panel_rows(panel):
        return pl.ds(pl.multiple_of(panel * columns, columns), columns)

    def take_factor(slot, panel):
        wait_bytes(part_of(slot, panel, (samp + 2) % n_samp), far_sem.at[slot, panel])
        wait_bytes(part_of(slot, panel, samp), own_sem.at[slot, panel])

    def update(slot, panel):
        take_factor(slot, panel)
        working[slot] -= dot_nt(solved[panel_rows(panel), :], gathered[slot, panel])

    def updates(slot, start, count):
        def body(step, carry):
            update(slot, start + step)
            return carry

        lax.fori_loop(0, count, body, 0)

    def take_samples(slot):
        wait_bytes(arrived.at[slot], sample_sem.at[slot])
        working[slot] = arrived[slot].astype(jnp.float32).reshape(columns, block)

    def send_rows(slot, piece):
        rows = pl.ds(pl.multiple_of(piece * chunk, chunk), chunk)
        value = working[slot, rows, :].reshape(ring, chunk // ring, block)
        leaving[slot, pl.ds(piece * ring, ring)] = value.astype(jnp.bfloat16)
        target = landed.at[slot, :, rows_of(me)]

        def body(step, carry):
            place = (2 * z + core + step) % ring
            to = at(place // 2, piece, place % 2)
            source = leaving.at[slot, piece * ring + place]

            @pl.when(to != me)
            def _():
                remote(source, target, sent_out, out_sem, to, samp)

            @pl.when(to == me)
            def _():
                pltpu.make_async_copy(source, target, out_sem).start()

            return carry

        lax.fori_loop(0, ring, body, 0)

    @pl.when(in_chain)
    def _():
        pltpu.make_async_copy(inverse_ref.at[0], inverse, inverse_sem).start()
        lax.fori_loop(0, me, send_direct, 0)
        send_near(1)

    @pl.when(jnp.logical_not(in_chain))
    def _():
        send_near(0)

    def send_rest():
        def body(step, carry):
            send_sample(0, plane + (me + step) % (n_rows - plane))
            return carry

        lax.fori_loop(0, n_rows - plane, body, 0)

    def send_second():
        def body(step, carry):
            send_sample(1, (me + step) % n_rows)
            return carry

        lax.fori_loop(0, n_rows, body, 0)

    def place_of(panel, piece):
        return pl.ds(pl.multiple_of(panel * columns + piece * chunk, chunk), chunk)

    def forward(panel, piece, sem, other):
        ref = solved.at[place_of(panel, piece)]
        remote(ref, ref, sem, solved_sem.at[panel, piece], other, samp)

    def forward_share(panel, piece, index, send_sem, recv_sem, other):
        start = panel * columns + piece * chunk + index * share
        ref = solved.at[pl.ds(pl.multiple_of(start, share), share)]
        remote(ref, ref, send_sem, recv_sem, other, samp)

    def receive(panel, piece):
        wait_bytes(solved.at[place_of(panel, piece)], solved_sem.at[panel, piece])

    def chain_item(index, carry):
        owner_x = x - (index // 2) % (x + 1)
        piece = (index // 2) // (x + 1) - owner_x
        panel = 2 * owner_x + index % 2
        rows = pl.ds(pl.multiple_of(piece * chunk, chunk), chunk)

        @pl.when((piece >= 0) & (piece < CHUNKS) & (panel <= me))
        def _():
            place = place_of(panel, piece)
            owner_core = panel % 2

            @pl.when(me == panel)
            def _():
                value = working[0, rows, :]
                high = value.astype(jnp.bfloat16)
                rest = value - high.astype(jnp.float32)
                middle = rest.astype(jnp.bfloat16)
                low = (rest - middle.astype(jnp.float32)).astype(jnp.bfloat16)
                product = dot_nt(jnp.concatenate([high, middle, low], axis=0), inverse[...])
                answer = product[:chunk] + (product[chunk : 2 * chunk] + product[2 * chunk :])
                working[0, rows, :] = answer
                solved[place, :] = answer.astype(jnp.bfloat16)

            @pl.when(me != panel)
            def _():
                receive(panel, piece)

            @pl.when((me == panel) | ((core == 0) & (owner_x < x)))
            def _():
                forward(panel, piece, sent_mate, mate)

            @pl.when((me == panel) & (core == 1))
            def _():
                for ahead in (1, 3, 2):
                    @pl.when(x + ahead < X_CHIPS)
                    def _():
                        forward(panel - 1, piece, sent_chain, at(z, x + ahead, 0))
                        forward(panel, piece, sent_chain, at(z, x + ahead, 0))

            @pl.when(me == panel)
            def _():
                for z_to in range(1, z_chips):
                    forward_share(
                        panel, piece, z_to, sent_share, share_sem.at[panel], at(z_to, piece, core)
                    )

                @pl.when(piece < x)
                def _():
                    forward_share(panel, piece, 0, sent_share, share_sem.at[panel], at(0, piece, core))

            @pl.when((piece == x) & (core == owner_core))
            def _():
                for z_to in range(1, z_chips):
                    forward_share(
                        panel, piece, 0, sent_z, solved_sem.at[panel, piece], at(z_to, x, core)
                    )
                for x_to in range(X_CHIPS - 1):
                    @pl.when(x_to < owner_x)
                    def _():
                        forward(panel, piece, sent_x, at(z, x_to, core))

            @pl.when(me > panel)
            def _():
                @pl.when(piece == 0)
                def _():
                    wait_bytes(gathered.at[0, panel], direct_sem.at[panel])

                working[0, rows, :] -= dot_nt(solved[place, :], gathered[0, panel])

        return carry

    first = jnp.where(in_chain, 2 * x + 2, 0)

    def parts(step):
        def with_panel(lag, body):
            panel = step - lag

            @pl.when((panel >= first) & (panel < panels))
            def _():
                body(panel, core == panel % 2, panel // 2)

        def give_share(panel, mine, owner_x):
            @pl.when(mine)
            def _():
                wait_bytes(solved.at[pl.ds(0, share)], share_sem.at[panel])
                for hop in range(1, z_chips):
                    z_to = (z + hop) % z_chips

                    @pl.when((z_to > 0) | (x < owner_x))
                    def _():
                        forward_share(
                            panel, x, z, sent_z, solved_sem.at[panel, x], at(z_to, x, core)
                        )

        def give_chunk(panel, mine, owner_x):
            @pl.when(mine)
            def _():
                wait_bytes(solved.at[pl.ds(0, chunk - share)], solved_sem.at[panel, x])
                for hop in (2, 1, 3):
                    x_to = (x + hop) % X_CHIPS

                    @pl.when((z > 0) | (x_to < owner_x))
                    def _():
                        forward(panel, x, sent_x, at(z, x_to, core))

                forward(panel, x, sent_mate, mate)

        def take_rest(panel, mine, owner_x):
            for hop in range(1, X_CHIPS):
                piece = (x + hop) % X_CHIPS
                receive(panel, piece)

                @pl.when(mine)
                def _():
                    forward(panel, piece, sent_mate, mate)

            @pl.when(jnp.logical_not(mine))
            def _():
                receive(panel, x)

        return with_panel, give_share, give_chunk, take_rest

    def spread_item(step, carry):
        with_panel, give_share, give_chunk, take_rest = parts(step)
        with_panel(0, give_share)
        with_panel(1, give_chunk)

        with_panel(2, take_rest)

        @pl.when(z > 0)
        def _():
            @pl.when(step < 2)
            def _():
                relays(0, panels // 2 * step, panels // 2)


            @pl.when(step == 1)
            def _():
                send_near(1)


            @pl.when(step == 4)
            def _():
                take_samples(0)
                updates(0, 0, 3)

            @pl.when(step > 4)
            def _():
                update(0, step - 2)

            @pl.when(step == 5)
            def _():
                relays(1, 0, 2)

            @pl.when(step > 5)
            def _():
                relays(1, 3 * step - 16, 3)

        return carry

    send_rest()
    send_second()

    @pl.when(in_chain)
    def _():
        wait_bytes(inverse, inverse_sem)
        take_samples(0)
        lax.fori_loop(0, 2 * (x + CHUNKS) * (x + 1), chain_item, 0)

        @pl.when(core == 0)
        def _():
            for piece in range(CHUNKS):
                receive(me + 1, piece)

    lax.fori_loop(0, panels, spread_item, 0)

    @pl.when(in_chain)
    def _():
        relays(1, 0, panels)

    last = panels - 1
    early = panels - 3
    with_panel, _, give_chunk, take_rest = parts(panels)
    take_samples(1)

    @pl.when(z > 0)
    def _():
        updates(1, 0, early)

    with_panel(1, give_chunk)
    with_panel(2, take_rest)

    @pl.when(z > 0)
    def _():
        update(0, last - 1)
        take_factor(0, last)

    @pl.when(z == 0)
    def _():
        updates(1, 0, early)

    updates(1, early, last - early)
    take_factor(1, last)

    def finish(hop, carry):
        piece = (x + hop) % X_CHIPS
        rows = pl.ds(pl.multiple_of(piece * chunk, chunk), chunk)
        mine = core == last % 2

        @pl.when((first <= last) & jnp.logical_not(mine & (piece == x)))
        def _():
            receive(last, piece)

        @pl.when((first <= last) & mine & (piece != x))
        def _():
            forward(last, piece, sent_mate, mate)

        @pl.when(z > 0)
        def _():
            working[0, rows, :] -= dot_nt(solved[place_of(last, piece), :], gathered[0, last])

        send_rows(0, piece)
        working[1, rows, :] -= dot_nt(solved[place_of(last, piece), :], gathered[1, last])
        send_rows(1, piece)
        return carry

    lax.fori_loop(0, CHUNKS, finish, 0)

    @pl.when(in_chain)
    def _():
        def sent(panel, carry):
            wait_bytes(gathered.at[0, 0, pl.ds(0, (n_samp - 1) * part), :], sent_direct.at[panel])
            return carry

        lax.fori_loop(0, me, sent, 0)
        wait_bytes(gathered.at[1, pl.ds(0, panels * 3 // n_samp)], sent_factor)

    def wait_rows(condition, rows, sem):
        if rows > 0:
            @pl.when(condition)
            def _():
                wait_bytes(solved.at[pl.ds(0, rows)], sem)

    wait_rows(z > 0, 16 * chunk, sent_mate)
    wait_rows(z > 0, 12 * chunk, sent_x)
    wait_rows(z == 0, 4 * (z_chips - 1) * share, sent_z)
    for place in range(X_CHIPS):
        here = in_chain & (x == place)
        wait_rows(here & (core == 0), 4 * (4 + place) * chunk, sent_mate)
        wait_rows(here & (core == 1), 4 * (4 - place) * chunk, sent_mate)
        wait_rows(here & (core == 1), 8 * (3 - place) * chunk, sent_chain)
        wait_rows(here, (3 + place) * chunk, sent_x)
        wait_rows(here, (4 * (z_chips - 1) + place) * share, sent_share)
        others = (z_chips - 1) * (3 - place) + (z_chips - 2) * (place + 1)
        wait_rows((z > 0) & (x == place), others * share, sent_z)

    @pl.when(jnp.logical_not(in_chain))
    def _():
        wait_bytes(gathered.at[:, pl.ds(0, panels * 3 // n_samp)], sent_factor)

    wait_bytes(arrived.at[:, pl.ds(0, n_rows - 1)], sent_sample)
    wait_bytes(leaving.at[:, pl.ds(0, n_rows - 1)], sent_out)
    wait_bytes(landed, out_sem)
    out_ref[...] = landed[...]


def local(samples, factor, diag_inverse):
    n_rows, n_samp = lax.axis_size("rows"), lax.axis_size("samp")
    slots, order, own = samples.shape
    block = diag_inverse.shape[2]
    panels = factor.shape[2] // block
    columns = own * n_rows
    result = pl.pallas_call(
        functools.partial(solve_kernel, n_rows, n_samp, panels),
        out_shape=jax.ShapeDtypeStruct((slots, own, order), jnp.bfloat16),
        in_specs=[pl.BlockSpec(memory_space=pl.ANY)] * 3,
        out_specs=pl.BlockSpec(memory_space=pltpu.VMEM),
        scratch_shapes=[
            pltpu.VMEM((slots, panels, block, block), jnp.bfloat16),
            pltpu.VMEM((panels * columns, block), jnp.bfloat16),
            pltpu.VMEM((slots, columns, block), jnp.float32),
            pltpu.VMEM((block, block), jnp.bfloat16),
            pltpu.VMEM((slots, n_rows, own, block), jnp.bfloat16),
            pltpu.VMEM((slots, n_rows, own, block), jnp.bfloat16),
            pltpu.VMEM((slots, own, order), jnp.bfloat16),
            pltpu.SemaphoreType.DMA((panels,)),
            pltpu.SemaphoreType.DMA((2, slots, panels)),
            pltpu.SemaphoreType.DMA((slots, panels)),
            pltpu.SemaphoreType.DMA((slots, panels)),
            pltpu.SemaphoreType.DMA((panels, CHUNKS)),
            pltpu.SemaphoreType.DMA((panels,)),
            pltpu.SemaphoreType.DMA((slots,)),
            pltpu.SemaphoreType.DMA((panels,)),
        ]
        + [pltpu.SemaphoreType.DMA] * 10,
        compiler_params=pltpu.CompilerParams(
            collective_id=0, has_side_effects=True, vmem_limit_bytes=60 * 2**20
        ),
    )(samples.transpose(0, 2, 1), factor, diag_inverse)
    return result.astype(jnp.float32).transpose(0, 2, 1)


def solution(mesh):
    placed = (
        P(None, None, ("rows", "samp")),
        P(None, ("rows", "samp"), None),
        P(None, "rows", None),
    )
    return jax.shard_map(
        local,
        mesh=mesh,
        in_specs=placed,
        out_specs=P(None, None, ("rows", "samp")),
        check_vma=False,
    )
```

```python
import functools

import jax
import jax.numpy as jnp
from jax import lax
from jax.experimental import pallas as pl
from jax.experimental.pallas import tpu as pltpu
from jax.sharding import PartitionSpec as P

MESH = pl.DeviceIdType.MESH
X_CHIPS = 4
CHUNKS = X_CHIPS
SLOTS = 2


def dot_nt(left, right):
    return lax.dot_general(
        left, right, (((1,), (1,)), ((), ())), preferred_element_type=jnp.float32
    )


def wait_bytes(ref, sem):
    pltpu.make_async_copy(ref, ref, sem).wait()


def solve_kernel(
    n_rows, n_samp, panels, sample_ref, factor_ref, inverse_ref, out_ref,
    gathered, solved, working, inverse, arrived, leaving, landed,
    direct_sem, near_sem, far_sem, own_sem, solved_sem, share_sem, sample_sem,
    sent_direct, sent_factor, sent_mate, sent_chain, sent_share, sent_x, sent_z, sent_sample, sent_out, out_sem,
    inverse_sem,
):
    block = inverse.shape[0]
    columns = working.shape[1]
    chunk = columns // CHUNKS
    part = block // n_samp
    plane = 2 * X_CHIPS
    z_chips = n_rows // plane
    share = chunk // z_chips
    me, samp = lax.axis_index("rows"), lax.axis_index("samp")
    z, x, core = me // plane, (me // 2) % X_CHIPS, me % 2
    in_chain = z == 0

    def at(z_to, x_to, core_to):
        return (z_to * X_CHIPS + x_to) * 2 + core_to

    mate = at(z, x, 1 - core)
    ring = 2 * z_chips
    group = x * ring + z * 2 + core

    def remote(source, target, send_sem, recv_sem, to_rows, to_samp):
        pltpu.make_async_remote_copy(
            src_ref=source, dst_ref=target, send_sem=send_sem, recv_sem=recv_sem,
            device_id=(to_rows, to_samp), device_id_type=MESH,
        ).start()

    barrier = pltpu.get_barrier_semaphore()

    def greet(step, carry):
        pl.semaphore_signal(
            barrier, inc=1, device_id=((me + step) % n_rows, samp), device_id_type=MESH
        )
        return carry

    lax.fori_loop(1, n_rows, greet, 0)
    for step in range(1, n_samp):
        pl.semaphore_signal(
            barrier, inc=1, device_id=(me, (samp + step) % n_samp), device_id_type=MESH
        )
    pl.semaphore_wait(barrier, n_rows + n_samp - 2)

    def rows_of(index):
        return pl.ds(pl.multiple_of(index * block, block), block)

    def send_sample(slot, to):
        source, target = sample_ref.at[slot, :, rows_of(to)], arrived.at[slot, group]

        @pl.when(to != me)
        def _():
            remote(source, target, sent_sample, sample_sem.at[slot], to, samp)

        @pl.when(to == me)
        def _():
            pltpu.make_async_copy(source, target, sample_sem.at[slot]).start()

    def send_window(to, carry):
        send_sample(0, to)
        return carry

    lax.fori_loop(0, plane, send_window, 0)

    def part_of(slot, panel, owner):
        return gathered.at[slot, panel, pl.ds(pl.multiple_of(owner * part, part), part), :]

    def own_part(slot, panel):
        return factor_ref.at[slot, :, rows_of(panel)]

    def send_direct(panel, carry):
        source, target = own_part(0, panel), part_of(0, panel, samp)
        pltpu.make_async_copy(source, target, direct_sem.at[panel]).start()
        for step in range(1, n_samp):
            remote(
                source, target, sent_direct.at[panel], direct_sem.at[panel],
                me, (samp + step) % n_samp,
            )
        return carry

    def send_near(slot):
        def body(panel, carry):
            source, target = own_part(slot, panel), part_of(slot, panel, samp)
            remote(source, target, sent_factor, near_sem.at[0, slot, panel], me, (samp + 1) % n_samp)
            remote(source, target, sent_factor, near_sem.at[1, slot, panel], me, (samp + 3) % n_samp)
            pltpu.make_async_copy(source, target, own_sem.at[slot, panel]).start()
            return carry

        lax.fori_loop(0, panels, body, 0)

    def relay(slot, panel):
        before, after = (samp + 3) % n_samp, (samp + 1) % n_samp
        from_before, from_after = part_of(slot, panel, before), part_of(slot, panel, after)
        wait_bytes(from_before, near_sem.at[0, slot, panel])
        wait_bytes(from_after, near_sem.at[1, slot, panel])

        @pl.when(panel % 2 == 0)
        def _():
            remote(from_before, from_before, sent_factor, far_sem.at[slot, panel], me, after)

        @pl.when(panel % 2 == 1)
        def _():
            remote(from_after, from_after, sent_factor, far_sem.at[slot, panel], me, before)

    def relays(slot, first, count):
        def body(step, carry):
            relay(slot, first + step)
            return carry

        lax.fori_loop(0, count, body, 0)

    def panel_rows(panel):
        return pl.ds(pl.multiple_of(panel * columns, columns), columns)

    def take_factor(slot, panel):
        wait_bytes(part_of(slot, panel, (samp + 2) % n_samp), far_sem.at[slot, panel])
        wait_bytes(part_of(slot, panel, samp), own_sem.at[slot, panel])

    def update(slot, panel):
        take_factor(slot, panel)
        working[slot] -= dot_nt(solved[panel_rows(panel), :], gathered[slot, panel])

    def updates(slot, start, count):
        def body(step, carry):
            update(slot, start + step)
            return carry

        lax.fori_loop(0, count, body, 0)

    def take_samples(slot):
        wait_bytes(arrived.at[slot], sample_sem.at[slot])
        working[slot] = arrived[slot].astype(jnp.float32).reshape(columns, block)

    def send_rows(slot, piece):
        rows = pl.ds(pl.multiple_of(piece * chunk, chunk), chunk)
        value = working[slot, rows, :].reshape(ring, chunk // ring, block)
        leaving[slot, pl.ds(piece * ring, ring)] = value.astype(jnp.bfloat16)
        target = landed.at[slot, :, rows_of(me)]

        def body(step, carry):
            place = (2 * z + core + step) % ring
            to = at(place // 2, piece, place % 2)
            source = leaving.at[slot, piece * ring + place]

            @pl.when(to != me)
            def _():
                remote(source, target, sent_out, out_sem, to, samp)

            @pl.when(to == me)
            def _():
                pltpu.make_async_copy(source, target, out_sem).start()

            return carry

        lax.fori_loop(0, ring, body, 0)

    @pl.when(in_chain)
    def _():
        pltpu.make_async_copy(inverse_ref.at[0], inverse, inverse_sem).start()
        lax.fori_loop(0, me, send_direct, 0)
        send_near(1)

    @pl.when(jnp.logical_not(in_chain))
    def _():
        send_near(0)

    def send_rest():
        def body(step, carry):
            send_sample(0, plane + (me + step) % (n_rows - plane))
            return carry

        lax.fori_loop(0, n_rows - plane, body, 0)

    def send_second():
        def body(step, carry):
            send_sample(1, (me + step) % n_rows)
            return carry

        lax.fori_loop(0, n_rows, body, 0)

    def place_of(panel, piece):
        return pl.ds(pl.multiple_of(panel * columns + piece * chunk, chunk), chunk)

    def forward(panel, piece, sem, other):
        ref = solved.at[place_of(panel, piece)]
        remote(ref, ref, sem, solved_sem.at[panel, piece], other, samp)

    def forward_share(panel, piece, index, send_sem, recv_sem, other):
        start = panel * columns + piece * chunk + index * share
        ref = solved.at[pl.ds(pl.multiple_of(start, share), share)]
        remote(ref, ref, send_sem, recv_sem, other, samp)

    def receive(panel, piece):
        wait_bytes(solved.at[place_of(panel, piece)], solved_sem.at[panel, piece])

    def chain_item(index, carry):
        owner_x = x - (index // 2) % (x + 1)
        piece = (index // 2) // (x + 1) - owner_x
        panel = 2 * owner_x + index % 2
        rows = pl.ds(pl.multiple_of(piece * chunk, chunk), chunk)

        @pl.when((piece >= 0) & (piece < CHUNKS) & (panel <= me))
        def _():
            place = place_of(panel, piece)
            owner_core = panel % 2

            @pl.when(me == panel)
            def _():
                value = working[0, rows, :]
                high = value.astype(jnp.bfloat16)
                rest = value - high.astype(jnp.float32)
                middle = rest.astype(jnp.bfloat16)
                low = (rest - middle.astype(jnp.float32)).astype(jnp.bfloat16)
                product = dot_nt(jnp.concatenate([high, middle, low], axis=0), inverse[...])
                answer = product[:chunk] + (product[chunk : 2 * chunk] + product[2 * chunk :])
                working[0, rows, :] = answer
                solved[place, :] = answer.astype(jnp.bfloat16)

            @pl.when(me != panel)
            def _():
                receive(panel, piece)

            @pl.when((me == panel) | ((core == 0) & (owner_x < x)))
            def _():
                forward(panel, piece, sent_mate, mate)

            @pl.when((me == panel) & (core == 1))
            def _():
                for ahead in (1, 3, 2):
                    @pl.when(x + ahead < X_CHIPS)
                    def _():
                        forward(panel - 1, piece, sent_chain, at(z, x + ahead, 0))
                        forward(panel, piece, sent_chain, at(z, x + ahead, 0))

            @pl.when(me == panel)
            def _():
                for z_to in range(1, z_chips):
                    forward_share(
                        panel, piece, z_to, sent_share, share_sem.at[panel], at(z_to, piece, core)
                    )

                @pl.when(piece < x)
                def _():
                    forward_share(panel, piece, 0, sent_share, share_sem.at[panel], at(0, piece, core))

            @pl.when((piece == x) & (core == owner_core))
            def _():
                for z_to in range(1, z_chips):
                    forward_share(
                        panel, piece, 0, sent_z, solved_sem.at[panel, piece], at(z_to, x, core)
                    )
                for x_to in range(X_CHIPS - 1):
                    @pl.when(x_to < owner_x)
                    def _():
                        forward(panel, piece, sent_x, at(z, x_to, core))

            @pl.when(me > panel)
            def _():
                @pl.when(piece == 0)
                def _():
                    wait_bytes(gathered.at[0, panel], direct_sem.at[panel])

                working[0, rows, :] -= dot_nt(solved[place, :], gathered[0, panel])

        return carry

    first = jnp.where(in_chain, 2 * x + 2, 0)

    def parts(step):
        def with_panel(lag, body):
            panel = step - lag

            @pl.when((panel >= first) & (panel < panels))
            def _():
                body(panel, core == panel % 2, panel // 2)

        def give_share(panel, mine, owner_x):
            @pl.when(mine)
            def _():
                wait_bytes(solved.at[pl.ds(0, share)], share_sem.at[panel])
                for hop in range(1, z_chips):
                    z_to = (z + hop) % z_chips

                    @pl.when((z_to > 0) | (x < owner_x))
                    def _():
                        forward_share(
                            panel, x, z, sent_z, solved_sem.at[panel, x], at(z_to, x, core)
                        )

        def give_chunk(panel, mine, owner_x):
            @pl.when(mine)
            def _():
                wait_bytes(solved.at[pl.ds(0, chunk - share)], solved_sem.at[panel, x])
                for hop in (2, 1, 3):
                    x_to = (x + hop) % X_CHIPS

                    @pl.when((z > 0) | (x_to < owner_x))
                    def _():
                        forward(panel, x, sent_x, at(z, x_to, core))

                forward(panel, x, sent_mate, mate)

        def take_rest(panel, mine, owner_x):
            for hop in range(1, X_CHIPS):
                piece = (x + hop) % X_CHIPS
                receive(panel, piece)

                @pl.when(mine)
                def _():
                    forward(panel, piece, sent_mate, mate)

            @pl.when(jnp.logical_not(mine))
            def _():
                receive(panel, x)

        return with_panel, give_share, give_chunk, take_rest

    def spread_item(step, carry):
        with_panel, give_share, give_chunk, take_rest = parts(step)
        with_panel(0, give_share)
        with_panel(1, give_chunk)

        with_panel(3, take_rest)

        @pl.when(z > 0)
        def _():
            @pl.when(step < 2)
            def _():
                relays(0, panels // 2 * step, panels // 2)


            @pl.when(step == 1)
            def _():
                send_near(1)


            @pl.when(step == 4)
            def _():
                take_samples(0)
                updates(0, 0, 2)

            @pl.when(step > 4)
            def _():
                update(0, step - 3)

            @pl.when(step == 5)
            def _():
                relays(1, 0, 2)

            @pl.when(step > 5)
            def _():
                relays(1, 3 * step - 16, 3)

        return carry

    send_rest()
    send_second()

    @pl.when(in_chain)
    def _():
        wait_bytes(inverse, inverse_sem)
        take_samples(0)
        lax.fori_loop(0, 2 * (x + CHUNKS) * (x + 1), chain_item, 0)

        @pl.when(core == 0)
        def _():
            for piece in range(CHUNKS):
                receive(me + 1, piece)

    lax.fori_loop(0, panels, spread_item, 0)

    @pl.when(in_chain)
    def _():
        relays(1, 0, panels)

    last = panels - 1
    early = panels - 4
    with_panel, _, give_chunk, take_rest = parts(panels)
    take_samples(1)

    @pl.when(z > 0)
    def _():
        updates(1, 0, early)

    with_panel(1, give_chunk)
    with_panel(3, take_rest)
    with_panel(2, take_rest)

    @pl.when(z > 0)
    def _():
        update(0, last - 2)
        update(0, last - 1)
        take_factor(0, last)

    @pl.when(z == 0)
    def _():
        updates(1, 0, early)

    updates(1, early, last - early)
    take_factor(1, last)

    def finish(hop, carry):
        piece = (x + hop) % X_CHIPS
        rows = pl.ds(pl.multiple_of(piece * chunk, chunk), chunk)
        mine = core == last % 2

        @pl.when((first <= last) & jnp.logical_not(mine & (piece == x)))
        def _():
            receive(last, piece)

        @pl.when((first <= last) & mine & (piece != x))
        def _():
            forward(last, piece, sent_mate, mate)

        @pl.when(z > 0)
        def _():
            working[0, rows, :] -= dot_nt(solved[place_of(last, piece), :], gathered[0, last])

        send_rows(0, piece)
        working[1, rows, :] -= dot_nt(solved[place_of(last, piece), :], gathered[1, last])
        send_rows(1, piece)
        return carry

    lax.fori_loop(0, CHUNKS, finish, 0)

    @pl.when(in_chain)
    def _():
        def sent(panel, carry):
            wait_bytes(gathered.at[0, 0, pl.ds(0, (n_samp - 1) * part), :], sent_direct.at[panel])
            return carry

        lax.fori_loop(0, me, sent, 0)
        wait_bytes(gathered.at[1, pl.ds(0, panels * 3 // n_samp)], sent_factor)

    def wait_rows(condition, rows, sem):
        if rows > 0:
            @pl.when(condition)
            def _():
                wait_bytes(solved.at[pl.ds(0, rows)], sem)

    wait_rows(z > 0, 16 * chunk, sent_mate)
    wait_rows(z > 0, 12 * chunk, sent_x)
    wait_rows(z == 0, 4 * (z_chips - 1) * share, sent_z)
    for place in range(X_CHIPS):
        here = in_chain & (x == place)
        wait_rows(here & (core == 0), 4 * (4 + place) * chunk, sent_mate)
        wait_rows(here & (core == 1), 4 * (4 - place) * chunk, sent_mate)
        wait_rows(here & (core == 1), 8 * (3 - place) * chunk, sent_chain)
        wait_rows(here, (3 + place) * chunk, sent_x)
        wait_rows(here, (4 * (z_chips - 1) + place) * share, sent_share)
        others = (z_chips - 1) * (3 - place) + (z_chips - 2) * (place + 1)
        wait_rows((z > 0) & (x == place), others * share, sent_z)

    @pl.when(jnp.logical_not(in_chain))
    def _():
        wait_bytes(gathered.at[:, pl.ds(0, panels * 3 // n_samp)], sent_factor)

    wait_bytes(arrived.at[:, pl.ds(0, n_rows - 1)], sent_sample)
    wait_bytes(leaving.at[:, pl.ds(0, n_rows - 1)], sent_out)
    wait_bytes(landed, out_sem)
    out_ref[...] = landed[...]


def local(samples, factor, diag_inverse):
    n_rows, n_samp = lax.axis_size("rows"), lax.axis_size("samp")
    slots, order, own = samples.shape
    block = diag_inverse.shape[2]
    panels = factor.shape[2] // block
    columns = own * n_rows
    result = pl.pallas_call(
        functools.partial(solve_kernel, n_rows, n_samp, panels),
        out_shape=jax.ShapeDtypeStruct((slots, own, order), jnp.bfloat16),
        in_specs=[pl.BlockSpec(memory_space=pl.ANY)] * 3,
        out_specs=pl.BlockSpec(memory_space=pltpu.VMEM),
        scratch_shapes=[
            pltpu.VMEM((slots, panels, block, block), jnp.bfloat16),
            pltpu.VMEM((panels * columns, block), jnp.bfloat16),
            pltpu.VMEM((slots, columns, block), jnp.float32),
            pltpu.VMEM((block, block), jnp.bfloat16),
            pltpu.VMEM((slots, n_rows, own, block), jnp.bfloat16),
            pltpu.VMEM((slots, n_rows, own, block), jnp.bfloat16),
            pltpu.VMEM((slots, own, order), jnp.bfloat16),
            pltpu.SemaphoreType.DMA((panels,)),
            pltpu.SemaphoreType.DMA((2, slots, panels)),
            pltpu.SemaphoreType.DMA((slots, panels)),
            pltpu.SemaphoreType.DMA((slots, panels)),
            pltpu.SemaphoreType.DMA((panels, CHUNKS)),
            pltpu.SemaphoreType.DMA((panels,)),
            pltpu.SemaphoreType.DMA((slots,)),
            pltpu.SemaphoreType.DMA((panels,)),
        ]
        + [pltpu.SemaphoreType.DMA] * 10,
        compiler_params=pltpu.CompilerParams(
            collective_id=0, has_side_effects=True, vmem_limit_bytes=60 * 2**20
        ),
    )(samples.transpose(0, 2, 1), factor, diag_inverse)
    return result.astype(jnp.float32).transpose(0, 2, 1)


def solution(mesh):
    placed = (
        P(None, None, ("rows", "samp")),
        P(None, ("rows", "samp"), None),
        P(None, "rows", None),
    )
    return jax.shard_map(
        local,
        mesh=mesh,
        in_specs=placed,
        out_specs=P(None, None, ("rows", "samp")),
        check_vma=False,
    )
```

```python
import functools

import jax
import jax.numpy as jnp
from jax import lax
from jax.experimental import pallas as pl
from jax.experimental.pallas import tpu as pltpu
from jax.sharding import PartitionSpec as P

MESH = pl.DeviceIdType.MESH
X_CHIPS = 4
CHUNKS = X_CHIPS
SLOTS = 2


def dot_nt(left, right):
    return lax.dot_general(
        left, right, (((1,), (1,)), ((), ())), preferred_element_type=jnp.float32
    )


def wait_bytes(ref, sem):
    pltpu.make_async_copy(ref, ref, sem).wait()


def solve_kernel(
    n_rows, n_samp, panels, sample_ref, factor_ref, inverse_ref, out_ref,
    gathered, solved, working, inverse, arrived, leaving, landed,
    direct_sem, near_sem, far_sem, own_sem, solved_sem, share_sem, sample_sem,
    sent_direct, sent_factor, sent_mate, sent_chain, sent_share, sent_x, sent_z, sent_sample, sent_out, out_sem,
    inverse_sem,
):
    block = inverse.shape[0]
    columns = working.shape[1]
    chunk = columns // CHUNKS
    part = block // n_samp
    plane = 2 * X_CHIPS
    z_chips = n_rows // plane
    share = chunk // z_chips
    me, samp = lax.axis_index("rows"), lax.axis_index("samp")
    z, x, core = me // plane, (me // 2) % X_CHIPS, me % 2
    in_chain = z == 0

    def at(z_to, x_to, core_to):
        return (z_to * X_CHIPS + x_to) * 2 + core_to

    mate = at(z, x, 1 - core)
    ring = 2 * z_chips
    group = x * ring + z * 2 + core

    def remote(source, target, send_sem, recv_sem, to_rows, to_samp):
        pltpu.make_async_remote_copy(
            src_ref=source, dst_ref=target, send_sem=send_sem, recv_sem=recv_sem,
            device_id=(to_rows, to_samp), device_id_type=MESH,
        ).start()

    barrier = pltpu.get_barrier_semaphore()

    def greet(step, carry):
        pl.semaphore_signal(
            barrier, inc=1, device_id=((me + step) % n_rows, samp), device_id_type=MESH
        )
        return carry

    lax.fori_loop(1, n_rows, greet, 0)
    for step in range(1, n_samp):
        pl.semaphore_signal(
            barrier, inc=1, device_id=(me, (samp + step) % n_samp), device_id_type=MESH
        )
    pl.semaphore_wait(barrier, n_rows + n_samp - 2)

    def rows_of(index):
        return pl.ds(pl.multiple_of(index * block, block), block)

    def send_sample(slot, to):
        source, target = sample_ref.at[slot, :, rows_of(to)], arrived.at[slot, group]

        @pl.when(to != me)
        def _():
            remote(source, target, sent_sample, sample_sem.at[slot], to, samp)

        @pl.when(to == me)
        def _():
            pltpu.make_async_copy(source, target, sample_sem.at[slot]).start()

    def send_window(to, carry):
        send_sample(0, to)
        return carry

    lax.fori_loop(0, plane, send_window, 0)

    def part_of(slot, panel, owner):
        return gathered.at[slot, panel, pl.ds(pl.multiple_of(owner * part, part), part), :]

    def own_part(slot, panel):
        return factor_ref.at[slot, :, rows_of(panel)]

    def send_direct(panel, carry):
        source, target = own_part(0, panel), part_of(0, panel, samp)
        pltpu.make_async_copy(source, target, direct_sem.at[panel]).start()
        for step in range(1, n_samp):
            remote(
                source, target, sent_direct.at[panel], direct_sem.at[panel],
                me, (samp + step) % n_samp,
            )
        return carry

    def send_near(slot):
        def body(panel, carry):
            source, target = own_part(slot, panel), part_of(slot, panel, samp)
            remote(source, target, sent_factor, near_sem.at[0, slot, panel], me, (samp + 1) % n_samp)
            remote(source, target, sent_factor, near_sem.at[1, slot, panel], me, (samp + 3) % n_samp)
            pltpu.make_async_copy(source, target, own_sem.at[slot, panel]).start()
            return carry

        lax.fori_loop(0, panels, body, 0)

    def relay(slot, panel):
        before, after = (samp + 3) % n_samp, (samp + 1) % n_samp
        from_before, from_after = part_of(slot, panel, before), part_of(slot, panel, after)
        wait_bytes(from_before, near_sem.at[0, slot, panel])
        wait_bytes(from_after, near_sem.at[1, slot, panel])

        @pl.when(panel % 2 == 0)
        def _():
            remote(from_before, from_before, sent_factor, far_sem.at[slot, panel], me, after)

        @pl.when(panel % 2 == 1)
        def _():
            remote(from_after, from_after, sent_factor, far_sem.at[slot, panel], me, before)

    def relays(slot, first, count):
        def body(step, carry):
            relay(slot, first + step)
            return carry

        lax.fori_loop(0, count, body, 0)

    def panel_rows(panel):
        return pl.ds(pl.multiple_of(panel * columns, columns), columns)

    def take_factor(slot, panel):
        wait_bytes(part_of(slot, panel, (samp + 2) % n_samp), far_sem.at[slot, panel])
        wait_bytes(part_of(slot, panel, samp), own_sem.at[slot, panel])

    def update(slot, panel):
        take_factor(slot, panel)
        working[slot] -= dot_nt(solved[panel_rows(panel), :], gathered[slot, panel])

    def updates(slot, start, count):
        def body(step, carry):
            update(slot, start + step)
            return carry

        lax.fori_loop(0, count, body, 0)

    def take_samples(slot):
        wait_bytes(arrived.at[slot], sample_sem.at[slot])
        working[slot] = arrived[slot].astype(jnp.float32).reshape(columns, block)

    def send_rows(slot, piece):
        rows = pl.ds(pl.multiple_of(piece * chunk, chunk), chunk)
        value = working[slot, rows, :].reshape(ring, chunk // ring, block)
        leaving[slot, pl.ds(piece * ring, ring)] = value.astype(jnp.bfloat16)
        target = landed.at[slot, :, rows_of(me)]

        def body(step, carry):
            place = (2 * z + core + step) % ring
            to = at(place // 2, piece, place % 2)
            source = leaving.at[slot, piece * ring + place]

            @pl.when(to != me)
            def _():
                remote(source, target, sent_out, out_sem, to, samp)

            @pl.when(to == me)
            def _():
                pltpu.make_async_copy(source, target, out_sem).start()

            return carry

        lax.fori_loop(0, ring, body, 0)

    @pl.when(in_chain)
    def _():
        pltpu.make_async_copy(inverse_ref.at[0], inverse, inverse_sem).start()
        lax.fori_loop(0, me, send_direct, 0)
        send_near(1)

    @pl.when(jnp.logical_not(in_chain))
    def _():
        send_near(0)

    def send_rest():
        def body(step, carry):
            send_sample(0, plane + (me + step) % (n_rows - plane))
            return carry

        lax.fori_loop(0, n_rows - plane, body, 0)

    def send_second():
        def body(step, carry):
            send_sample(1, (me + step) % n_rows)
            return carry

        lax.fori_loop(0, n_rows, body, 0)

    def place_of(panel, piece):
        return pl.ds(pl.multiple_of(panel * columns + piece * chunk, chunk), chunk)

    def forward(panel, piece, sem, other):
        ref = solved.at[place_of(panel, piece)]
        remote(ref, ref, sem, solved_sem.at[panel, piece], other, samp)

    def forward_share(panel, piece, index, send_sem, recv_sem, other):
        start = panel * columns + piece * chunk + index * share
        ref = solved.at[pl.ds(pl.multiple_of(start, share), share)]
        remote(ref, ref, send_sem, recv_sem, other, samp)

    def receive(panel, piece):
        wait_bytes(solved.at[place_of(panel, piece)], solved_sem.at[panel, piece])

    def chain_item(index, carry):
        owner_x = x - (index // 2) % (x + 1)
        piece = (index // 2) // (x + 1) - owner_x
        panel = 2 * owner_x + index % 2
        rows = pl.ds(pl.multiple_of(piece * chunk, chunk), chunk)

        @pl.when((piece >= 0) & (piece < CHUNKS) & (panel <= me))
        def _():
            place = place_of(panel, piece)
            owner_core = panel % 2

            @pl.when(me == panel)
            def _():
                value = working[0, rows, :]
                high = value.astype(jnp.bfloat16)
                rest = value - high.astype(jnp.float32)
                middle = rest.astype(jnp.bfloat16)
                low = (rest - middle.astype(jnp.float32)).astype(jnp.bfloat16)
                product = dot_nt(jnp.concatenate([high, middle, low], axis=0), inverse[...])
                answer = product[:chunk] + (product[chunk : 2 * chunk] + product[2 * chunk :])
                working[0, rows, :] = answer
                solved[place, :] = answer.astype(jnp.bfloat16)

            @pl.when(me != panel)
            def _():
                receive(panel, piece)

            @pl.when((me == panel) | ((core == 0) & (owner_x < x)))
            def _():
                forward(panel, piece, sent_mate, mate)

            @pl.when((me == panel) & (core == 1))
            def _():
                for ahead in (1, 2, 3):
                    @pl.when(x + ahead < X_CHIPS)
                    def _():
                        forward(panel - 1, piece, sent_chain, at(z, x + ahead, 0))
                        forward(panel, piece, sent_chain, at(z, x + ahead, 0))

            @pl.when(me == panel)
            def _():
                for z_to in range(1, z_chips):
                    forward_share(
                        panel, piece, z_to, sent_share, share_sem.at[panel], at(z_to, piece, core)
                    )

                @pl.when(piece < x)
                def _():
                    forward_share(panel, piece, 0, sent_share, share_sem.at[panel], at(0, piece, core))

            @pl.when((piece == x) & (core == owner_core))
            def _():
                for z_to in range(1, z_chips):
                    forward_share(
                        panel, piece, 0, sent_z, solved_sem.at[panel, piece], at(z_to, x, core)
                    )
                for x_to in range(X_CHIPS - 1):
                    @pl.when(x_to < owner_x)
                    def _():
                        forward(panel, piece, sent_x, at(z, x_to, core))

            @pl.when(me > panel)
            def _():
                @pl.when(piece == 0)
                def _():
                    wait_bytes(gathered.at[0, panel], direct_sem.at[panel])

                working[0, rows, :] -= dot_nt(solved[place, :], gathered[0, panel])

        return carry

    first = jnp.where(in_chain, 2 * x + 2, 0)

    def parts(step):
        def with_panel(lag, body):
            panel = step - lag

            @pl.when((panel >= first) & (panel < panels))
            def _():
                body(panel, core == panel % 2, panel // 2)

        def give_share(panel, mine, owner_x):
            @pl.when(mine)
            def _():
                wait_bytes(solved.at[pl.ds(0, share)], share_sem.at[panel])
                for hop in range(1, z_chips):
                    z_to = (z + hop) % z_chips

                    @pl.when((z_to > 0) | (x < owner_x))
                    def _():
                        forward_share(
                            panel, x, z, sent_z, solved_sem.at[panel, x], at(z_to, x, core)
                        )

        def give_chunk(panel, mine, owner_x):
            @pl.when(mine)
            def _():
                wait_bytes(solved.at[pl.ds(0, chunk - share)], solved_sem.at[panel, x])
                for hop in (2, 1, 3):
                    x_to = (x + hop) % X_CHIPS

                    @pl.when((z > 0) | (x_to < owner_x))
                    def _():
                        forward(panel, x, sent_x, at(z, x_to, core))

                forward(panel, x, sent_mate, mate)

        def take_rest(panel, mine, owner_x):
            for hop in range(1, X_CHIPS):
                piece = (x + hop) % X_CHIPS
                receive(panel, piece)

                @pl.when(mine)
                def _():
                    forward(panel, piece, sent_mate, mate)

            @pl.when(jnp.logical_not(mine))
            def _():
                receive(panel, x)

        return with_panel, give_share, give_chunk, take_rest

    def spread_item(step, carry):
        with_panel, give_share, give_chunk, take_rest = parts(step)
        with_panel(0, give_share)
        with_panel(1, give_chunk)

        with_panel(3, take_rest)

        @pl.when(z > 0)
        def _():
            @pl.when(step < 2)
            def _():
                relays(0, panels // 2 * step, panels // 2)


            @pl.when(step == 1)
            def _():
                send_near(1)


            @pl.when(step == 4)
            def _():
                take_samples(0)
                updates(0, 0, 2)

            @pl.when(step > 4)
            def _():
                update(0, step - 3)

            @pl.when(step == 5)
            def _():
                relays(1, 0, 2)

            @pl.when(step > 5)
            def _():
                relays(1, 3 * step - 16, 3)

        return carry

    send_rest()
    send_second()

    @pl.when(in_chain)
    def _():
        wait_bytes(inverse, inverse_sem)
        take_samples(0)
        lax.fori_loop(0, 2 * (x + CHUNKS) * (x + 1), chain_item, 0)

        @pl.when(core == 0)
        def _():
            for piece in range(CHUNKS):
                receive(me + 1, piece)

    lax.fori_loop(0, panels, spread_item, 0)

    @pl.when(in_chain)
    def _():
        relays(1, 0, panels)

    last = panels - 1
    early = panels - 4
    with_panel, _, give_chunk, take_rest = parts(panels)
    take_samples(1)

    @pl.when(z > 0)
    def _():
        updates(1, 0, early)

    with_panel(1, give_chunk)
    with_panel(3, take_rest)
    with_panel(2, take_rest)

    @pl.when(z > 0)
    def _():
        update(0, last - 2)
        update(0, last - 1)
        take_factor(0, last)

    @pl.when(z == 0)
    def _():
        updates(1, 0, early)

    updates(1, early, last - early)
    take_factor(1, last)

    def finish(hop, carry):
        piece = (x + hop) % X_CHIPS
        rows = pl.ds(pl.multiple_of(piece * chunk, chunk), chunk)
        mine = core == last % 2

        @pl.when((first <= last) & jnp.logical_not(mine & (piece == x)))
        def _():
            receive(last, piece)

        @pl.when((first <= last) & mine & (piece != x))
        def _():
            forward(last, piece, sent_mate, mate)

        @pl.when(z > 0)
        def _():
            working[0, rows, :] -= dot_nt(solved[place_of(last, piece), :], gathered[0, last])

        send_rows(0, piece)
        working[1, rows, :] -= dot_nt(solved[place_of(last, piece), :], gathered[1, last])
        send_rows(1, piece)
        return carry

    lax.fori_loop(0, CHUNKS, finish, 0)

    @pl.when(in_chain)
    def _():
        def sent(panel, carry):
            wait_bytes(gathered.at[0, 0, pl.ds(0, (n_samp - 1) * part), :], sent_direct.at[panel])
            return carry

        lax.fori_loop(0, me, sent, 0)
        wait_bytes(gathered.at[1, pl.ds(0, panels * 3 // n_samp)], sent_factor)

    def wait_rows(condition, rows, sem):
        if rows > 0:
            @pl.when(condition)
            def _():
                wait_bytes(solved.at[pl.ds(0, rows)], sem)

    wait_rows(z > 0, 16 * chunk, sent_mate)
    wait_rows(z > 0, 12 * chunk, sent_x)
    wait_rows(z == 0, 4 * (z_chips - 1) * share, sent_z)
    for place in range(X_CHIPS):
        here = in_chain & (x == place)
        wait_rows(here & (core == 0), 4 * (4 + place) * chunk, sent_mate)
        wait_rows(here & (core == 1), 4 * (4 - place) * chunk, sent_mate)
        wait_rows(here & (core == 1), 8 * (3 - place) * chunk, sent_chain)
        wait_rows(here, (3 + place) * chunk, sent_x)
        wait_rows(here, (4 * (z_chips - 1) + place) * share, sent_share)
        others = (z_chips - 1) * (3 - place) + (z_chips - 2) * (place + 1)
        wait_rows((z > 0) & (x == place), others * share, sent_z)

    @pl.when(jnp.logical_not(in_chain))
    def _():
        wait_bytes(gathered.at[:, pl.ds(0, panels * 3 // n_samp)], sent_factor)

    wait_bytes(arrived.at[:, pl.ds(0, n_rows - 1)], sent_sample)
    wait_bytes(leaving.at[:, pl.ds(0, n_rows - 1)], sent_out)
    wait_bytes(landed, out_sem)
    out_ref[...] = landed[...]


def local(samples, factor, diag_inverse):
    n_rows, n_samp = lax.axis_size("rows"), lax.axis_size("samp")
    slots, order, own = samples.shape
    block = diag_inverse.shape[2]
    panels = factor.shape[2] // block
    columns = own * n_rows
    result = pl.pallas_call(
        functools.partial(solve_kernel, n_rows, n_samp, panels),
        out_shape=jax.ShapeDtypeStruct((slots, own, order), jnp.bfloat16),
        in_specs=[pl.BlockSpec(memory_space=pl.ANY)] * 3,
        out_specs=pl.BlockSpec(memory_space=pltpu.VMEM),
        scratch_shapes=[
            pltpu.VMEM((slots, panels, block, block), jnp.bfloat16),
            pltpu.VMEM((panels * columns, block), jnp.bfloat16),
            pltpu.VMEM((slots, columns, block), jnp.float32),
            pltpu.VMEM((block, block), jnp.bfloat16),
            pltpu.VMEM((slots, n_rows, own, block), jnp.bfloat16),
            pltpu.VMEM((slots, n_rows, own, block), jnp.bfloat16),
            pltpu.VMEM((slots, own, order), jnp.bfloat16),
            pltpu.SemaphoreType.DMA((panels,)),
            pltpu.SemaphoreType.DMA((2, slots, panels)),
            pltpu.SemaphoreType.DMA((slots, panels)),
            pltpu.SemaphoreType.DMA((slots, panels)),
            pltpu.SemaphoreType.DMA((panels, CHUNKS)),
            pltpu.SemaphoreType.DMA((panels,)),
            pltpu.SemaphoreType.DMA((slots,)),
            pltpu.SemaphoreType.DMA((panels,)),
        ]
        + [pltpu.SemaphoreType.DMA] * 10,
        compiler_params=pltpu.CompilerParams(
            collective_id=0, has_side_effects=True, vmem_limit_bytes=60 * 2**20
        ),
    )(samples.transpose(0, 2, 1), factor, diag_inverse)
    return result.astype(jnp.float32).transpose(0, 2, 1)


def solution(mesh):
    placed = (
        P(None, None, ("rows", "samp")),
        P(None, ("rows", "samp"), None),
        P(None, "rows", None),
    )
    return jax.shard_map(
        local,
        mesh=mesh,
        in_specs=placed,
        out_specs=P(None, None, ("rows", "samp")),
        check_vma=False,
    )
```
